32 devices in a mesh: parts: 2 (over y), shard: 4 (over z), blk: 2 (over x), rep: 2 (over core).
Axes of the slice: x: 2, y: 2, z: 4, core: 2. Of those that a mesh axis runs over, the one named last changes fastest.
Arguments:
- embeddings: bfloat16 [4096, 1024], P(('parts', 'shard', 'blk', 'rep')), parts along dimension 0
- row_cluster: int32 [4096], P(('parts', 'shard', 'blk', 'rep')), parts along dimension 0, may hold values from 0 to 255, as said below
- cluster_sizes: int32 [512], P('parts'), parts along dimension 0, may hold values from 512 to 8192
Outputs:
- neighbour_mean: bfloat16 [4096, 1024], P(('parts', 'shard', 'blk', 'rep')), parts along dimension 0
- density: bfloat16 [4096], P(('parts', 'shard', 'blk', 'rep')), parts along dimension 0
The draws below stay inside these ranges and needn't reach their ends.
There are 2 independent parts, one for each index of `parts`. The reference program is written for one: setup_inputs(seed, part) draws one part's arguments, and reference() takes and returns one part's arrays. A program takes and returns all parts, laid end to end along the dimension named above; each array names one. Nothing has to cross between parts.
Inputs may be any that keep to these rules, and one draw needn't show every extreme that they name: `row_cluster`: clusters d * 64 to (d + 1) * 64 - 1 are owned by subgroup d. At most 48 documents of one device (an aligned block of 128 documents) lie in the clusters of one subgroup; in every draw some subgroup receives exactly 48 documents from every device. Of the documents of one device in the clusters of one subgroup, at most 12 have clusters with one and the same index modulo 2 * 2; in every draw some subgroup and some such index receive exactly 12 from every device.
All inputs are finite; a program needn't handle non-finite values.
Results may differ from the reference program's by a relative error of at most 0.0045.
Values may be sent and summed in bfloat16 or wider, within the bound.
A program may use at most 64 MiB of HBM per device.

```python
import math
import jax
import jax.numpy as jnp
from jax import lax

D = 1024
ROW_DEV = 128
CLU_SUB = 64
OWNER_SUBSETS = 4
ROWS = 2048
NCLUST = 256
CAP = 48
KEYS = 768
N_BLK = 2
N_REP = 2


def cluster_draw(key):
    initial_random_key = jax.random.fold_in(key, 101)
    popular_cluster_key, reward_random_key, noise_random_key, device_random_key, round_random_key = jax.random.split(initial_random_key, 5)
    devices = ROWS // ROW_DEV
    members = N_BLK * N_REP
    hottest = jax.random.randint(popular_cluster_key, (), 0, OWNER_SUBSETS)
    reward_terms = jax.random.randint(reward_random_key, (OWNER_SUBSETS,), 0, 2 ** 17)
    reward_terms = reward_terms + jnp.where(jnp.arange(OWNER_SUBSETS) == hottest, 2 ** 18, 0)
    jitter = jax.random.randint(noise_random_key, (devices, OWNER_SUBSETS, CAP), 0, 2 ** 16)
    slot_index = jnp.arange(OWNER_SUBSETS * CAP, dtype=jnp.int32).reshape(OWNER_SUBSETS, CAP)
    scores = (jitter + reward_terms[None, :, None]) * 2048 + slot_index[None, :, :]
    top_values, picked = lax.top_k(scores.reshape(devices, OWNER_SUBSETS * CAP).astype(jnp.int32), ROW_DEV)
    owners = picked // CAP
    slot_place = picked % CAP
    turns = jax.random.randint(round_random_key, (OWNER_SUBSETS,), 0, members)
    member = (slot_place + turns[owners]) % members
    local_index = member + members * jax.random.randint(device_random_key, (devices, ROW_DEV), 0, CLU_SUB // members)
    return (owners * CLU_SUB + local_index).reshape(ROWS).astype(jnp.int32)


def draw_row_cluster(key, part):
    return cluster_draw(key)


def draw_embeddings(key, part):
    cluster_ids = cluster_draw(key)
    initial_random_key = jax.random.fold_in(key, 7)
    keys_list = jax.random.split(initial_random_key, 5)
    centroids = jax.random.normal(keys_list[0], (NCLUST, D), jnp.float32)
    column_scale = jnp.exp(jax.random.uniform(keys_list[4], (1, D), jnp.float32, math.log(0.3), math.log(3.0)))
    strength = jnp.exp(jax.random.uniform(keys_list[1], (ROWS, 1), jnp.float32, 0.0, math.log(3.0)))
    jitter = jax.random.normal(keys_list[2], (ROWS, D), jnp.float32)
    row_scale = jnp.exp(jax.random.uniform(keys_list[3], (ROWS, 1), jnp.float32, math.log(0.5), math.log(2.0)))
    mixed = (strength * centroids[cluster_ids] + jitter) / jnp.sqrt(strength * strength + 1.0)
    return (mixed * column_scale * row_scale).astype(jnp.bfloat16)


def with_ends(entries, rng, low, largest):
    shape = entries.shape
    place = [jax.random.randint(jax.random.fold_in(rng, axis), (), 0, shape[axis]) for axis in range(len(shape))]
    entries = entries.at[tuple(place)].set(low)
    longest = shape.index(max(shape))
    place[longest] = (place[longest] + 1) % shape[longest]
    return entries.at[tuple(place)].set(largest)


def setup_inputs(seed: int = 0, part: int = 0) -> dict:
    streams_of = jax.random.split(jax.random.key(seed), 4)
    part_splits = jax.random.split(jax.random.fold_in(streams_of[3], part), 4)
    return {
        "embeddings": draw_embeddings(jax.random.fold_in(jax.random.fold_in(streams_of[3], part), 71), part),
        "row_cluster": draw_row_cluster(jax.random.fold_in(jax.random.fold_in(streams_of[3], part), 71), part),
        "cluster_sizes": with_ends(jax.random.randint(part_splits[2], (NCLUST,), 512, 8193), jax.random.fold_in(part_splits[2], 1), 512, 8192).astype(jnp.int32),
    }


temper = 8.0
unit_count = 1024.0
tiny_eps = 1e-06

def inverse_norms(row_block):
    widened = row_block.astype(jnp.float32)
    return lax.rsqrt(lax.optimization_barrier(jnp.sum(widened * widened, axis=1)) + tiny_eps)

def neighbour_stats(group_rows, group_ids, cluster_sizes):
    inverse = inverse_norms(group_rows)
    products = jnp.dot(group_rows, group_rows.T, preferred_element_type=jnp.float32)
    cosine = products * inverse[:, None] * inverse[None, :]
    matched = (group_ids[:, None] == group_ids[None, :]) & (group_ids[None, :] >= 0)
    kernel = jnp.where(matched, jnp.exp(temper * (cosine - 1.0)), 0.0)
    size_rows = jnp.where(group_ids >= 0, cluster_sizes[jnp.maximum(group_ids, 0)], 1).astype(jnp.float32)
    density = (lax.optimization_barrier(jnp.sum(kernel, axis=1)) * (unit_count / size_rows)).astype(jnp.bfloat16)
    weights = (kernel * density.astype(jnp.float32)[None, :]).astype(jnp.bfloat16)
    numerator = jnp.dot(weights, group_rows, preferred_element_type=jnp.float32)
    denominator = lax.optimization_barrier(jnp.sum(weights.astype(jnp.float32), axis=1))
    denominator = jnp.where(group_ids >= 0, denominator, 1.0)
    return ((numerator / denominator[:, None]).astype(jnp.bfloat16), density)

def reference(embeddings, row_cluster, cluster_sizes):
    owners = (row_cluster // CLU_SUB).astype(jnp.int32)
    row_order = jnp.argsort(owners, stable=True).astype(jnp.int32)
    counts = lax.optimization_barrier(jnp.sum((owners[:, None] == jnp.arange(OWNER_SUBSETS, dtype=jnp.int32)[None, :]).astype(jnp.int32), axis=0)).astype(jnp.int32)
    starts = (jnp.cumsum(counts) - counts).astype(jnp.int32)
    sorted_rows = jnp.concatenate([embeddings[row_order], jnp.zeros((KEYS, D), embeddings.dtype)], axis=0)
    sorted_ids = jnp.concatenate([row_cluster[row_order].astype(jnp.int32), jnp.full((KEYS,), -1, jnp.int32)], axis=0)
    positions = jnp.arange(KEYS, dtype=jnp.int32)

    def one_group(group_index):
        group_start = starts[group_index].astype(jnp.int32)
        group_rows = lax.dynamic_slice_in_dim(sorted_rows, group_start, KEYS, 0)
        group_ids = lax.dynamic_slice_in_dim(sorted_ids, group_start, KEYS, 0)
        group_ids = jnp.where(positions < counts[group_index], group_ids, -1).astype(jnp.int32)
        return neighbour_stats(group_rows, group_ids, cluster_sizes)
    group_means, group_density = lax.map(one_group, jnp.arange(OWNER_SUBSETS, dtype=jnp.int32))
    sorted_owner = owners[row_order]
    within = (jnp.arange(ROWS, dtype=jnp.int32) - starts[sorted_owner]).astype(jnp.int32)
    mean_sorted = group_means[sorted_owner, within]
    density_sorted = group_density[sorted_owner, within]
    neighbour_mean = jnp.zeros((ROWS, D), mean_sorted.dtype).at[row_order].set(mean_sorted)
    density = jnp.zeros((ROWS,), density_sorted.dtype).at[row_order].set(density_sorted)
    return (neighbour_mean, density)
```

```python
import functools

import jax
import jax.numpy as jnp
from jax import lax
from jax.experimental import pallas as pl
from jax.experimental.pallas import tpu as pltpu
from jax.sharding import PartitionSpec as P

CLU_SUB = 64
TILE = 16

temper = 8.0
unit_count = 1024.0
tiny_eps = 1e-06

f32 = jnp.float32
bf16 = jnp.bfloat16
i32 = jnp.int32
MESH = pl.DeviceIdType.MESH


def dot(a, b, dims=((1,), (0,))):
    return lax.dot_general(a, b, (dims, ((), ())), preferred_element_type=f32)


def iota(shape, dim):
    return lax.broadcasted_iota(i32, shape, dim)


def one_hot(hits):
    return jnp.where(hits, 1.0, 0.0).astype(bf16)


def to_column(row):
    n = row.shape[1]
    eye = iota((n, n), 0) == iota((n, n), 1)
    return jnp.sum(jnp.where(eye, row, jnp.zeros_like(row)), axis=1, keepdims=True)


def to_row(column):
    n = column.shape[0]
    eye = iota((n, n), 0) == iota((n, n), 1)
    return jnp.sum(jnp.where(eye, column, jnp.zeros_like(column)), axis=0, keepdims=True)


def log2(value):
    assert value & (value - 1) == 0
    return value.bit_length() - 1


def kernel(
    sizes, cap,
    emb_ref, ids_ref, counts_ref, mean_ref, dens_ref,
    packed, owned, reply, returned, id_out, id_in, dens_out, dens_in,
    id_send, id_recv, row_send, row_recv, dens_send, dens_recv, back_send, back_recv,
):
    shards, blks, reps = sizes
    members = blks * reps
    devices = shards * members
    rows, width = emb_ref.shape
    slots = devices * TILE
    spare = TILE - cap
    groups = cap // spare
    side = width // TILE * spare
    main = width - side

    shard = lax.axis_index("shard")
    member = lax.axis_index("blk") * reps + lax.axis_index("rep")
    me = shard * members + member

    def partner(step):
        other, place, at, left = 0, 1, me, step
        while place < devices:
            other = other + ((at + left % 2) % 2) * place
            at, left, place = at // 2, left // 2, place * 2
        return other

    def device(index):
        return {"shard": index // members, "blk": index // reps % blks, "rep": index % reps}

    order = list(range(devices - 1, 0, -1))
    barrier = pltpu.get_barrier_semaphore()
    for step in order:
        pl.semaphore_signal(barrier, inc=1, device_id=device(partner(step)), device_id_type=MESH)

    def chunk(ref, index):
        return ref.at[pl.ds(pl.multiple_of(index * TILE, TILE), TILE), :]

    ids = ids_ref[...]
    owner = (ids >> log2(CLU_SUB)) * members + (ids & (members - 1))
    local = (ids & (CLU_SUB - 1)) >> log2(members)
    owner_col = to_column(owner)
    earlier = iota((rows, rows), 0) < iota((rows, rows), 1)
    same = owner_col == owner
    rank = jnp.sum(jnp.where(same & earlier, 1, 0), axis=0, keepdims=True)
    rank_third = sum(jnp.where(rank >= groups * q, 1, 0) for q in range(1, spare))
    rank_group = rank - groups * rank_third
    target = owner * TILE + rank
    side_target = owner * TILE + cap + rank_third

    slot_index = iota((slots, rows), 0)
    place = one_hot(slot_index == target)
    side_place = [
        one_hot(slot_index == jnp.where(rank_group == g, side_target, -1)) for g in range(groups)
    ]
    id_out[...] = dot((local + 1).astype(f32).astype(bf16), place, ((1,), (1,)))
    last = emb_ref[:, main:]
    for g in range(groups):
        columns = slice(g * side, (g + 1) * side)
        both = jnp.concatenate([place, side_place[g]], axis=1)
        stacked = jnp.concatenate([emb_ref[:, columns], last], axis=0)
        packed[:, columns] = dot(both, stacked).astype(bf16)

    pl.semaphore_wait(barrier, devices - 1)

    def remote(src, dst, send, recv, index):
        return pltpu.make_async_remote_copy(
            src_ref=src, dst_ref=dst, send_sem=send, recv_sem=recv,
            device_id=device(index), device_id_type=MESH,
        )

    for step in order:
        remote(id_out, id_in.at[me], id_send, id_recv, partner(step)).start()
    for step in order:
        other = partner(step)
        remote(chunk(packed, other), chunk(owned, me), row_send, row_recv, other).start()
    own_ids = pltpu.make_async_copy(id_out, id_in.at[me], id_recv)
    own_ids.start()
    own_rows = pltpu.make_async_copy(chunk(packed, me), chunk(owned, me), row_recv)
    own_rows.start()

    def wait_all(ref, sem):
        pltpu.make_async_copy(ref, ref, sem).wait()

    def wait_sent(ref, sem):
        part = ref.at[pl.ds(0, ref.shape[0] // devices * (devices - 1))]
        pltpu.make_async_copy(part, part, sem).wait()

    pick = one_hot(iota((slots, slots), 0) == me * TILE + (iota((slots, slots), 1) & (TILE - 1)))
    mine = iota((devices, slots), 0) == (iota((devices, slots), 1) >> log2(TILE))

    def for_me(table):
        stacked = jnp.concatenate([table[d] for d in range(devices)], axis=0).astype(bf16)
        return jnp.sum(jnp.where(mine, dot(stacked, pick), 0.0), axis=0, keepdims=True)

    wait_all(id_in, id_recv)
    slot_id = for_me(id_in)
    slot_id_col = to_column(slot_id)
    matched = (slot_id_col == slot_id) & (slot_id > 0.0)
    cluster = shard * CLU_SUB + (slot_id_col.astype(i32) - 1) * members + member
    cluster = jnp.where(slot_id_col > 0.0, cluster, -1)
    counts = counts_ref[...]
    table_hits = cluster == iota((slots, counts.shape[1]), 1)
    size = jnp.sum(jnp.where(table_hits, counts, 0), axis=1, keepdims=True)
    size_factor = unit_count / jnp.where(cluster >= 0, size, 1).astype(f32)
    eye = iota((slots, slots), 0) == iota((slots, slots), 1)
    row_place = iota((slots, slots), 0) & (TILE - 1)
    same_tile = (iota((slots, slots), 0) >> log2(TILE)) == (iota((slots, slots), 1) >> log2(TILE))
    column_place = iota((slots, slots), 1) & (TILE - 1)
    unfold = [
        one_hot(same_tile & (column_place >= cap) & (row_place == (column_place - cap) * groups + g))
        for g in range(groups)
    ]
    fold = [
        one_hot(same_tile & (row_place >= cap) & (column_place == (row_place - cap) * groups + g))
        for g in range(groups)
    ]

    wait_all(owned, row_recv)
    docs = owned[...]
    docs_side = sum(
        dot(unfold[g], docs[:, g * side:(g + 1) * side]) for g in range(groups)
    ).astype(bf16)
    gram = dot(docs, docs, ((1,), (1,))) + dot(docs_side, docs_side, ((1,), (1,)))
    diagonal = jnp.where(eye, gram, 0.0)
    scale_col = lax.rsqrt(jnp.sum(diagonal, axis=1, keepdims=True) + tiny_eps)
    scale_row = lax.rsqrt(jnp.sum(diagonal, axis=0, keepdims=True) + tiny_eps)
    cosine = gram * scale_col * scale_row
    values = jnp.where(matched, jnp.exp(temper * (cosine - 1.0)), 0.0)
    density = (jnp.sum(values, axis=1, keepdims=True) * size_factor).astype(bf16).astype(f32)
    density = to_row(density)
    dens_out[...] = density
    weights = (values * density).astype(bf16)
    denominator = jnp.sum(weights.astype(f32), axis=1, keepdims=True)
    denominator = jnp.where(slot_id_col > 0.0, denominator, 1.0)
    mean_side = (dot(weights, docs_side) / denominator).astype(bf16)
    for g in range(groups):
        columns = slice(g * side, (g + 1) * side)
        mean_main = dot(weights, docs[:, columns]) / denominator
        reply[:, columns] = (mean_main + dot(fold[g], mean_side)).astype(bf16)

    for step in order:
        other = partner(step)
        remote(chunk(reply, other), chunk(returned, me), back_send, back_recv, other).start()
    for step in order:
        remote(dens_out, dens_in.at[me], dens_send, dens_recv, partner(step)).start()
    own_back = pltpu.make_async_copy(chunk(reply, me), chunk(returned, me), back_recv)
    own_back.start()
    own_dens = pltpu.make_async_copy(dens_out, dens_in.at[me], dens_recv)
    own_dens.start()

    target_col = to_column(target)
    side_target_col = to_column(side_target)
    group_col = to_column(rank_group)
    lane = iota((rows, slots), 1)
    take = one_hot(lane == target_col)
    take_side = [
        one_hot(lane == jnp.where(group_col == g, side_target_col, -1)) for g in range(groups)
    ]
    wait_sent(id_in, id_send)
    wait_sent(packed, row_send)
    wait_all(dens_in, dens_recv)
    dens_ref[...] = dot(for_me(dens_in).astype(bf16), place).astype(dens_ref.dtype)
    wait_all(returned, back_recv)
    back = returned[...]
    mean_ref[:, :main] = dot(take, back).astype(bf16)
    mean_ref[:, main:] = sum(
        dot(take_side[g], back[:, g * side:(g + 1) * side]) for g in range(groups)
    ).astype(bf16)
    wait_sent(reply, back_send)
    wait_sent(dens_in, dens_send)


def with_kernel(sizes, cap, embeddings, row_cluster, cluster_sizes):
    devices = sizes[0] * sizes[1] * sizes[2]
    rows, width = embeddings.shape
    slots = devices * TILE
    main = width // TILE * cap
    wide = pltpu.VMEM((slots, main), bf16)
    line = pltpu.VMEM((1, slots), f32)
    lines = pltpu.VMEM((devices, 1, slots), f32)
    mean, density = pl.pallas_call(
        functools.partial(kernel, sizes, cap),
        out_shape=(
            jax.ShapeDtypeStruct((rows, width), bf16),
            jax.ShapeDtypeStruct((1, rows), f32),
        ),
        in_specs=[pl.BlockSpec(memory_space=pltpu.VMEM)] * 3,
        out_specs=(pl.BlockSpec(memory_space=pltpu.VMEM),) * 2,
        scratch_shapes=[wide, wide, wide, wide, line, lines, line, lines]
        + [pltpu.SemaphoreType.DMA] * 8,
        compiler_params=pltpu.CompilerParams(
            collective_id=0, has_side_effects=True, vmem_limit_bytes=32 * 1024 * 1024
        ),
    )(embeddings, row_cluster[None, :], cluster_sizes[None, :])
    return mean, density[0].astype(bf16)


def with_exchange(sizes, cap, embeddings, row_cluster, cluster_sizes):
    axes = ("shard", "blk", "rep")
    members = sizes[1] * sizes[2]
    devices = sizes[0] * members
    slots = devices * cap
    owner = row_cluster // CLU_SUB * members + row_cluster % members
    same = owner[:, None] == owner[None, :]
    position = jnp.arange(owner.shape[0], dtype=i32)
    rank = jnp.sum((same & (position[None, :] < position[:, None])).astype(i32), axis=1)
    placing = (owner * cap + rank)[None, :] == jnp.arange(slots, dtype=i32)[:, None]
    packed = dot(placing.astype(bf16), embeddings).astype(bf16)
    packed_ids = jnp.sum(jnp.where(placing, row_cluster[None, :] + 1, 0), axis=1) - 1

    def exchange(array):
        return lax.all_to_all(array, axes, split_axis=0, concat_axis=0, tiled=True)

    docs, ids = exchange(packed), exchange(packed_ids)
    wide = docs.astype(f32)
    scale = lax.rsqrt(jnp.sum(wide * wide, axis=1) + tiny_eps)
    cosine = dot(docs, docs, ((1,), (1,))) * scale[:, None] * scale[None, :]
    matched = (ids[:, None] == ids[None, :]) & (ids[None, :] >= 0)
    values = jnp.where(matched, jnp.exp(temper * (cosine - 1.0)), 0.0)
    hits = ids[:, None] == jnp.arange(cluster_sizes.shape[0], dtype=i32)[None, :]
    size = jnp.sum(jnp.where(hits, cluster_sizes[None, :], 0), axis=1)
    size = jnp.where(ids >= 0, size, 1).astype(f32)
    density = (jnp.sum(values, axis=1) * (unit_count / size)).astype(bf16)
    weights = (values * density.astype(f32)[None, :]).astype(bf16)
    denominator = jnp.sum(weights.astype(f32), axis=1)
    denominator = jnp.where(ids >= 0, denominator, 1.0)
    mean = (dot(weights, docs) / denominator[:, None]).astype(bf16)
    back, back_density = exchange(mean), exchange(density)
    rows_out = dot(placing.astype(bf16), back, ((0,), (0,))).astype(bf16)
    density_out = jnp.sum(jnp.where(placing, back_density.astype(f32)[:, None], 0.0), axis=0)
    return rows_out, density_out.astype(bf16)


def on_device(sizes, embeddings, row_cluster, cluster_sizes):
    rows, width = embeddings.shape
    devices = sizes[0] * sizes[1] * sizes[2]
    cap = -(-3 * rows // (2 * devices))
    spare = TILE - cap
    foldable = spare > 0 and cap % spare == 0 and width * spare % (TILE * 128) == 0
    small = devices & (devices - 1) == 0 and devices <= 32
    run = with_kernel if foldable and small else with_exchange
    return run(sizes, cap, embeddings, row_cluster, cluster_sizes)


def solution(mesh):
    sizes = tuple(mesh.shape[name] for name in ("shard", "blk", "rep"))
    return jax.shard_map(
        functools.partial(on_device, sizes),
        mesh=mesh,
        in_specs=(
            P(("parts", "shard", "blk", "rep"), None),
            P(("parts", "shard", "blk", "rep")),
            P("parts"),
        ),
        out_specs=(P(("parts", "shard", "blk", "rep"), None), P(("parts", "shard", "blk", "rep"))),
        check_vma=False,
    )
```

```python
import functools

import jax
import jax.numpy as jnp
from jax import lax
from jax.experimental import pallas as pl
from jax.experimental.pallas import tpu as pltpu
from jax.sharding import PartitionSpec as P

CLU_SUB = 64
TILE = 16

temper = 8.0
unit_count = 1024.0
tiny_eps = 1e-06

f32 = jnp.float32
bf16 = jnp.bfloat16
i32 = jnp.int32
MESH = pl.DeviceIdType.MESH


def dot(a, b, dims=((1,), (0,))):
    return lax.dot_general(a, b, (dims, ((), ())), preferred_element_type=f32)


def iota(shape, dim):
    return lax.broadcasted_iota(i32, shape, dim)


def one_hot(hits):
    return jnp.where(hits, 1.0, 0.0).astype(bf16)


def to_column(row):
    n = row.shape[1]
    eye = iota((n, n), 0) == iota((n, n), 1)
    return jnp.sum(jnp.where(eye, row, jnp.zeros_like(row)), axis=1, keepdims=True)


def to_row(column):
    n = column.shape[0]
    eye = iota((n, n), 0) == iota((n, n), 1)
    return jnp.sum(jnp.where(eye, column, jnp.zeros_like(column)), axis=0, keepdims=True)


def log2(value):
    assert value & (value - 1) == 0
    return value.bit_length() - 1


def kernel(
    sizes, cap,
    emb_hbm, ids_hbm, counts_hbm, mean_ref, dens_ref,
    emb_ref, ids_ref, counts_ref, packed, owned, reply, returned, id_out, id_in, dens_out, dens_in,
    emb_in, ids_in, counts_in, id_send, id_recv, row_send, row_recv, dens_send, dens_recv, back_send, back_recv,
):
    shards, blks, reps = sizes
    members = blks * reps
    devices = shards * members
    rows, width = emb_ref.shape
    slots = devices * TILE
    spare = TILE - cap
    groups = cap // spare
    side = width // TILE * spare
    main = width - side

    shard = lax.axis_index("shard")
    member = lax.axis_index("blk") * reps + lax.axis_index("rep")
    me = shard * members + member

    def partner(step):
        other, place, at, left = 0, 1, me, step
        while place < devices:
            other = other + ((at + left % 2) % 2) * place
            at, left, place = at // 2, left // 2, place * 2
        return other

    def device(index):
        return {"shard": index // members, "blk": index // reps % blks, "rep": index % reps}

    half = devices // 2
    order = list(range(devices - 1, 0, -1))
    order = [step for pair in zip(order, order[half:]) for step in pair] + [half]

    ids_copy = pltpu.make_async_copy(ids_hbm, ids_ref, ids_in)
    emb_copy = pltpu.make_async_copy(emb_hbm, emb_ref, emb_in)
    counts_copy = pltpu.make_async_copy(counts_hbm, counts_ref, counts_in)
    ids_copy.start()
    emb_copy.start()
    counts_copy.start()

    barrier = pltpu.get_barrier_semaphore()
    for step in order:
        pl.semaphore_signal(barrier, inc=1, device_id=device(partner(step)), device_id_type=MESH)

    def chunk(ref, index):
        return ref.at[pl.ds(pl.multiple_of(index * TILE, TILE), TILE), :]

    ids_copy.wait()
    ids = ids_ref[...]
    owner = (ids >> log2(CLU_SUB)) * members + (ids & (members - 1))
    local = (ids & (CLU_SUB - 1)) >> log2(members)
    owner_col = to_column(owner)
    earlier = iota((rows, rows), 0) < iota((rows, rows), 1)
    same = owner_col == owner
    rank = jnp.sum(jnp.where(same & earlier, 1, 0), axis=0, keepdims=True)
    rank_third = sum(jnp.where(rank >= groups * q, 1, 0) for q in range(1, spare))
    rank_group = rank - groups * rank_third
    target = owner * TILE + rank
    side_target = owner * TILE + cap + rank_third

    place = one_hot(iota((slots, rows), 0) == target)
    id_out[...] = dot((local + 1).astype(f32).astype(bf16), place, ((1,), (1,)))

    def remote(src, dst, send, recv, index):
        return pltpu.make_async_remote_copy(
            src_ref=src, dst_ref=dst, send_sem=send, recv_sem=recv,
            device_id=device(index), device_id_type=MESH,
        )

    emb_copy.wait()
    last = emb_ref[:, main:]
    slot_index = iota((slots, rows), 0)
    for g in range(groups):
        columns = slice(g * side, (g + 1) * side)
        there = one_hot(slot_index == jnp.where(rank_group == g, side_target, -1))
        both = jnp.concatenate([place, there], axis=1)
        stacked = jnp.concatenate([emb_ref[:, columns], last], axis=0)
        packed[:, columns] = dot(both, stacked).astype(bf16)
    pl.semaphore_wait(barrier, devices - 1)
    for step in order:
        remote(id_out, id_in.at[me], id_send, id_recv, partner(step)).start()
    for step in order:
        other = partner(step)
        remote(chunk(packed, other), chunk(owned, me), row_send, row_recv, other).start()
    own_ids = pltpu.make_async_copy(id_out, id_in.at[me], id_recv)
    own_ids.start()
    own_rows = pltpu.make_async_copy(chunk(packed, me), chunk(owned, me), row_recv)
    own_rows.start()

    def wait_all(ref, sem):
        pltpu.make_async_copy(ref, ref, sem).wait()

    def wait_sent(ref, sem):
        part = ref.at[pl.ds(0, ref.shape[0] // devices * (devices - 1))]
        pltpu.make_async_copy(part, part, sem).wait()

    pick = one_hot(iota((slots, slots), 0) == me * TILE + (iota((slots, slots), 1) & (TILE - 1)))
    mine = iota((devices, slots), 0) == (iota((devices, slots), 1) >> log2(TILE))

    def for_me(table):
        stacked = jnp.concatenate([table[d] for d in range(devices)], axis=0).astype(bf16)
        return jnp.sum(jnp.where(mine, dot(stacked, pick), 0.0), axis=0, keepdims=True)

    wait_all(id_in, id_recv)
    slot_id = for_me(id_in)
    slot_id_col = to_column(slot_id)
    matched = (slot_id_col == slot_id) & (slot_id > 0.0)
    cluster = shard * CLU_SUB + (slot_id_col.astype(i32) - 1) * members + member
    cluster = jnp.where(slot_id_col > 0.0, cluster, -1)
    counts_copy.wait()
    counts = counts_ref[...]
    table_hits = cluster == iota((slots, counts.shape[1]), 1)
    size = jnp.sum(jnp.where(table_hits, counts, 0), axis=1, keepdims=True)
    size_factor = unit_count / jnp.where(cluster >= 0, size, 1).astype(f32)
    eye = iota((slots, slots), 0) == iota((slots, slots), 1)
    row_place = iota((slots, slots), 0) & (TILE - 1)
    same_tile = (iota((slots, slots), 0) >> log2(TILE)) == (iota((slots, slots), 1) >> log2(TILE))
    column_place = iota((slots, slots), 1) & (TILE - 1)
    unfold = [
        one_hot(same_tile & (column_place >= cap) & (row_place == (column_place - cap) * groups + g))
        for g in range(groups)
    ]
    fold = [
        one_hot(same_tile & (row_place >= cap) & (column_place == (row_place - cap) * groups + g))
        for g in range(groups)
    ]

    wait_all(owned, row_recv)
    docs = owned[...]
    docs_side = sum(
        dot(unfold[g], docs[:, g * side:(g + 1) * side]) for g in range(groups)
    ).astype(bf16)
    gram = dot(docs, docs, ((1,), (1,))) + dot(docs_side, docs_side, ((1,), (1,)))
    diagonal = jnp.where(eye, gram, 0.0)
    scale_col = lax.rsqrt(jnp.sum(diagonal, axis=1, keepdims=True) + tiny_eps)
    scale_row = lax.rsqrt(jnp.sum(diagonal, axis=0, keepdims=True) + tiny_eps)
    cosine = gram * scale_col * scale_row
    values = jnp.where(matched, jnp.exp(temper * (cosine - 1.0)), 0.0)
    density = (jnp.sum(values, axis=1, keepdims=True) * size_factor).astype(bf16).astype(f32)
    density = to_row(density)
    dens_out[...] = density
    weights = (values * density).astype(bf16)
    denominator = jnp.sum(weights.astype(f32), axis=1, keepdims=True)
    denominator = jnp.where(slot_id_col > 0.0, denominator, 1.0)
    inverse = 1.0 / denominator
    mean_side = (dot(weights, docs_side) * inverse).astype(bf16)
    for g in range(groups):
        columns = slice(g * side, (g + 1) * side)
        mean_main = dot(weights, docs[:, columns]) * inverse
        reply[:, columns] = (mean_main + dot(fold[g], mean_side)).astype(bf16)
    for step in order:
        other = partner(step)
        remote(chunk(reply, other), chunk(returned, me), back_send, back_recv, other).start()
    for step in order:
        remote(dens_out, dens_in.at[me], dens_send, dens_recv, partner(step)).start()
    own_back = pltpu.make_async_copy(chunk(reply, me), chunk(returned, me), back_recv)
    own_back.start()
    own_dens = pltpu.make_async_copy(dens_out, dens_in.at[me], dens_recv)
    own_dens.start()

    target_col = to_column(target)
    side_target_col = to_column(side_target)
    group_col = to_column(rank_group)
    lane = iota((rows, slots), 1)
    take = one_hot(lane == target_col)
    take_side = [
        one_hot(lane == jnp.where(group_col == g, side_target_col, -1)) for g in range(groups)
    ]
    wait_sent(id_in, id_send)
    wait_sent(packed, row_send)
    wait_all(dens_in, dens_recv)
    dens_ref[...] = dot(for_me(dens_in).astype(bf16), place).astype(dens_ref.dtype)
    wait_all(returned, back_recv)
    back = returned[...]
    mean_ref[:, :main] = dot(take, back).astype(bf16)
    mean_ref[:, main:] = sum(
        dot(take_side[g], back[:, g * side:(g + 1) * side]) for g in range(groups)
    ).astype(bf16)
    wait_sent(reply, back_send)
    wait_sent(dens_in, dens_send)


def with_kernel(sizes, cap, embeddings, row_cluster, cluster_sizes):
    devices = sizes[0] * sizes[1] * sizes[2]
    rows, width = embeddings.shape
    slots = devices * TILE
    main = width // TILE * cap
    wide = pltpu.VMEM((slots, main), bf16)
    operands = embeddings, row_cluster[None, :], cluster_sizes[None, :]
    line = pltpu.VMEM((1, slots), f32)
    lines = pltpu.VMEM((devices, 1, slots), f32)
    mean, density = pl.pallas_call(
        functools.partial(kernel, sizes, cap),
        out_shape=(
            jax.ShapeDtypeStruct((rows, width), bf16),
            jax.ShapeDtypeStruct((1, rows), f32),
        ),
        in_specs=[pl.BlockSpec(memory_space=pltpu.HBM)] * 3,
        out_specs=(pl.BlockSpec(memory_space=pltpu.VMEM),) * 2,
        scratch_shapes=[
            pltpu.VMEM((rows, width), bf16),
            pltpu.VMEM((1, rows), i32),
            pltpu.VMEM((1, cluster_sizes.shape[0]), i32),
        ]
        + [wide, wide, wide, wide, line, lines, line, lines]
        + [pltpu.SemaphoreType.DMA] * 11,
        compiler_params=pltpu.CompilerParams(
            collective_id=0, has_side_effects=True, vmem_limit_bytes=32 * 1024 * 1024
        ),
    )(*(pltpu.with_memory_space_constraint(a, pltpu.HBM) for a in operands))
    return mean, density[0].astype(bf16)


def with_exchange(sizes, cap, embeddings, row_cluster, cluster_sizes):
    axes = ("shard", "blk", "rep")
    members = sizes[1] * sizes[2]
    devices = sizes[0] * members
    slots = devices * cap
    owner = row_cluster // CLU_SUB * members + row_cluster % members
    same = owner[:, None] == owner[None, :]
    position = jnp.arange(owner.shape[0], dtype=i32)
    rank = jnp.sum((same & (position[None, :] < position[:, None])).astype(i32), axis=1)
    placing = (owner * cap + rank)[None, :] == jnp.arange(slots, dtype=i32)[:, None]
    packed = dot(placing.astype(bf16), embeddings).astype(bf16)
    packed_ids = jnp.sum(jnp.where(placing, row_cluster[None, :] + 1, 0), axis=1) - 1

    def exchange(array):
        return lax.all_to_all(array, axes, split_axis=0, concat_axis=0, tiled=True)

    docs, ids = exchange(packed), exchange(packed_ids)
    wide = docs.astype(f32)
    scale = lax.rsqrt(jnp.sum(wide * wide, axis=1) + tiny_eps)
    cosine = dot(docs, docs, ((1,), (1,))) * scale[:, None] * scale[None, :]
    matched = (ids[:, None] == ids[None, :]) & (ids[None, :] >= 0)
    values = jnp.where(matched, jnp.exp(temper * (cosine - 1.0)), 0.0)
    hits = ids[:, None] == jnp.arange(cluster_sizes.shape[0], dtype=i32)[None, :]
    size = jnp.sum(jnp.where(hits, cluster_sizes[None, :], 0), axis=1)
    size = jnp.where(ids >= 0, size, 1).astype(f32)
    density = (jnp.sum(values, axis=1) * (unit_count / size)).astype(bf16)
    weights = (values * density.astype(f32)[None, :]).astype(bf16)
    denominator = jnp.sum(weights.astype(f32), axis=1)
    denominator = jnp.where(ids >= 0, denominator, 1.0)
    mean = (dot(weights, docs) / denominator[:, None]).astype(bf16)
    back, back_density = exchange(mean), exchange(density)
    rows_out = dot(placing.astype(bf16), back, ((0,), (0,))).astype(bf16)
    density_out = jnp.sum(jnp.where(placing, back_density.astype(f32)[:, None], 0.0), axis=0)
    return rows_out, density_out.astype(bf16)


def on_device(sizes, embeddings, row_cluster, cluster_sizes):
    rows, width = embeddings.shape
    devices = sizes[0] * sizes[1] * sizes[2]
    cap = -(-3 * rows // (2 * devices))
    spare = TILE - cap
    foldable = spare > 0 and cap % spare == 0 and width * spare % (TILE * 128) == 0
    small = devices & (devices - 1) == 0 and devices <= 32
    run = with_kernel if foldable and small else with_exchange
    return run(sizes, cap, embeddings, row_cluster, cluster_sizes)


def solution(mesh):
    sizes = tuple(mesh.shape[name] for name in ("shard", "blk", "rep"))
    return jax.shard_map(
        functools.partial(on_device, sizes),
        mesh=mesh,
        in_specs=(
            P(("parts", "shard", "blk", "rep"), None),
            P(("parts", "shard", "blk", "rep")),
            P("parts"),
        ),
        out_specs=(P(("parts", "shard", "blk", "rep"), None), P(("parts", "shard", "blk", "rep"))),
        check_vma=False,
    )
```

```python
import functools

import jax
import jax.numpy as jnp
from jax import lax
from jax.experimental import pallas as pl
from jax.experimental.pallas import tpu as pltpu
from jax.sharding import PartitionSpec as P

CLU_SUB = 64
TILE = 16

temper = 8.0
unit_count = 1024.0
tiny_eps = 1e-06

f32 = jnp.float32
bf16 = jnp.bfloat16
i32 = jnp.int32
MESH = pl.DeviceIdType.MESH


def dot(a, b, dims=((1,), (0,))):
    return lax.dot_general(a, b, (dims, ((), ())), preferred_element_type=f32)


def iota(shape, dim):
    return lax.broadcasted_iota(i32, shape, dim)


def one_hot(hits):
    return jnp.where(hits, 1.0, 0.0).astype(bf16)


def to_column(row):
    n = row.shape[1]
    eye = iota((n, n), 0) == iota((n, n), 1)
    return jnp.sum(jnp.where(eye, row, jnp.zeros_like(row)), axis=1, keepdims=True)


def to_row(column):
    n = column.shape[0]
    eye = iota((n, n), 0) == iota((n, n), 1)
    return jnp.sum(jnp.where(eye, column, jnp.zeros_like(column)), axis=0, keepdims=True)


def log2(value):
    assert value & (value - 1) == 0
    return value.bit_length() - 1


def kernel(
    sizes, cap,
    emb_hbm, ids_hbm, counts_hbm, mean_ref, dens_ref,
    emb_ref, ids_ref, counts_ref, packed, owned, reply, returned, id_out, id_in, dens_out, dens_in,
    emb_in, ids_in, counts_in, id_send, id_recv, row_send, row_recv, dens_send, dens_recv, back_send, back_recv,
):
    shards, blks, reps = sizes
    members = blks * reps
    devices = shards * members
    rows, width = emb_ref.shape
    slots = devices * TILE
    spare = TILE - cap
    groups = cap // spare
    side = width // TILE * spare
    main = width - side

    shard = lax.axis_index("shard")
    member = lax.axis_index("blk") * reps + lax.axis_index("rep")
    me = shard * members + member

    def partner(step):
        other, place, at, left = 0, 1, me // reps, step
        while place < devices // reps:
            other = other + ((at + left % 2) % 2) * place
            at, left, place = at // 2, left // 2, place * 2
        return other * reps

    def device(index):
        return {"shard": index // members, "blk": index // reps % blks, "rep": index % reps}

    chips = devices // reps
    steps = list(range(chips - 1, 0, -1))
    steps = [step for pair in zip(steps, steps[chips // 2:]) for step in pair] + [chips // 2]
    rep = lax.axis_index("rep")
    others = [me // reps * reps + (rep + r) % reps for r in range(1, reps)]
    others += [partner(step) + r for r in range(reps) for step in steps]

    ids_copy = pltpu.make_async_copy(ids_hbm, ids_ref, ids_in)
    emb_copy = pltpu.make_async_copy(emb_hbm, emb_ref, emb_in)
    counts_copy = pltpu.make_async_copy(counts_hbm, counts_ref, counts_in)
    ids_copy.start()
    emb_copy.start()
    counts_copy.start()

    barrier = pltpu.get_barrier_semaphore()
    for other in others:
        pl.semaphore_signal(barrier, inc=1, device_id=device(other), device_id_type=MESH)

    def chunk(ref, index):
        return ref.at[pl.ds(pl.multiple_of(index * TILE, TILE), TILE), :]

    ids_copy.wait()
    ids = ids_ref[...]
    owner = (ids >> log2(CLU_SUB)) * members + (ids & (members - 1))
    local = (ids & (CLU_SUB - 1)) >> log2(members)
    owner_col = to_column(owner)
    earlier = iota((rows, rows), 0) < iota((rows, rows), 1)
    same = owner_col == owner
    rank = jnp.sum(jnp.where(same & earlier, 1, 0), axis=0, keepdims=True)
    rank_third = sum(jnp.where(rank >= groups * q, 1, 0) for q in range(1, spare))
    rank_group = rank - groups * rank_third
    target = owner * TILE + rank
    side_target = owner * TILE + cap + rank_third

    place = one_hot(iota((slots, rows), 0) == target)
    id_out[...] = dot((local + 1).astype(f32).astype(bf16), place, ((1,), (1,)))

    def remote(src, dst, send, recv, index):
        return pltpu.make_async_remote_copy(
            src_ref=src, dst_ref=dst, send_sem=send, recv_sem=recv,
            device_id=device(index), device_id_type=MESH,
        )

    emb_copy.wait()
    last = emb_ref[:, main:]
    slot_index = iota((slots, rows), 0)
    for g in range(groups):
        columns = slice(g * side, (g + 1) * side)
        there = one_hot(slot_index == jnp.where(rank_group == g, side_target, -1))
        both = jnp.concatenate([place, there], axis=1)
        stacked = jnp.concatenate([emb_ref[:, columns], last], axis=0)
        packed[:, columns] = dot(both, stacked).astype(bf16)
    pl.semaphore_wait(barrier, devices - 1)
    for other in others:
        remote(id_out, id_in.at[me], id_send, id_recv, other).start()
    for other in others:
        remote(chunk(packed, other), chunk(owned, me), row_send, row_recv, other).start()
    own_ids = pltpu.make_async_copy(id_out, id_in.at[me], id_recv)
    own_ids.start()
    own_rows = pltpu.make_async_copy(chunk(packed, me), chunk(owned, me), row_recv)
    own_rows.start()

    def wait_all(ref, sem):
        pltpu.make_async_copy(ref, ref, sem).wait()

    def wait_sent(ref, sem):
        part = ref.at[pl.ds(0, ref.shape[0] // devices * (devices - 1))]
        pltpu.make_async_copy(part, part, sem).wait()

    pick = one_hot(iota((slots, slots), 0) == me * TILE + (iota((slots, slots), 1) & (TILE - 1)))
    mine = iota((devices, slots), 0) == (iota((devices, slots), 1) >> log2(TILE))

    def for_me(table):
        stacked = jnp.concatenate([table[d] for d in range(devices)], axis=0).astype(bf16)
        return jnp.sum(jnp.where(mine, dot(stacked, pick), 0.0), axis=0, keepdims=True)

    wait_all(id_in, id_recv)
    slot_id = for_me(id_in)
    slot_id_col = to_column(slot_id)
    matched = (slot_id_col == slot_id) & (slot_id > 0.0)
    cluster = shard * CLU_SUB + (slot_id_col.astype(i32) - 1) * members + member
    cluster = jnp.where(slot_id_col > 0.0, cluster, -1)
    counts_copy.wait()
    counts = counts_ref[...]
    table_hits = cluster == iota((slots, counts.shape[1]), 1)
    size = jnp.sum(jnp.where(table_hits, counts, 0), axis=1, keepdims=True)
    size_factor = unit_count / jnp.where(cluster >= 0, size, 1).astype(f32)
    eye = iota((slots, slots), 0) == iota((slots, slots), 1)
    row_place = iota((slots, slots), 0) & (TILE - 1)
    same_tile = (iota((slots, slots), 0) >> log2(TILE)) == (iota((slots, slots), 1) >> log2(TILE))
    column_place = iota((slots, slots), 1) & (TILE - 1)
    unfold = [
        one_hot(same_tile & (column_place >= cap) & (row_place == (column_place - cap) * groups + g))
        for g in range(groups)
    ]
    fold = [
        one_hot(same_tile & (row_place >= cap) & (column_place == (row_place - cap) * groups + g))
        for g in range(groups)
    ]

    wait_all(owned, row_recv)
    docs = owned[...]
    docs_side = sum(
        dot(unfold[g], docs[:, g * side:(g + 1) * side]) for g in range(groups)
    ).astype(bf16)
    gram = dot(docs, docs, ((1,), (1,))) + dot(docs_side, docs_side, ((1,), (1,)))
    diagonal = jnp.where(eye, gram, 0.0)
    scale_col = lax.rsqrt(jnp.sum(diagonal, axis=1, keepdims=True) + tiny_eps)
    scale_row = lax.rsqrt(jnp.sum(diagonal, axis=0, keepdims=True) + tiny_eps)
    cosine = gram * scale_col * scale_row
    values = jnp.where(matched, jnp.exp(temper * (cosine - 1.0)), 0.0)
    density = (jnp.sum(values, axis=1, keepdims=True) * size_factor).astype(bf16).astype(f32)
    density = to_row(density)
    dens_out[...] = density
    weights = (values * density).astype(bf16)
    denominator = jnp.sum(weights.astype(f32), axis=1, keepdims=True)
    denominator = jnp.where(slot_id_col > 0.0, denominator, 1.0)
    inverse = 1.0 / denominator
    for other in others:
        remote(dens_out, dens_in.at[me], dens_send, dens_recv, other).start()
    mean_side = (dot(weights, docs_side) * inverse).astype(bf16)
    for g in range(groups):
        columns = slice(g * side, (g + 1) * side)
        mean_main = dot(weights, docs[:, columns]) * inverse
        reply[:, columns] = (mean_main + dot(fold[g], mean_side)).astype(bf16)
    for other in others:
        remote(chunk(reply, other), chunk(returned, me), back_send, back_recv, other).start()
    own_back = pltpu.make_async_copy(chunk(reply, me), chunk(returned, me), back_recv)
    own_back.start()
    own_dens = pltpu.make_async_copy(dens_out, dens_in.at[me], dens_recv)
    own_dens.start()

    target_col = to_column(target)
    side_target_col = to_column(side_target)
    group_col = to_column(rank_group)
    lane = iota((rows, slots), 1)
    take = one_hot(lane == target_col)
    take_side = [
        one_hot(lane == jnp.where(group_col == g, side_target_col, -1)) for g in range(groups)
    ]
    wait_sent(id_in, id_send)
    wait_sent(packed, row_send)
    wait_all(dens_in, dens_recv)
    dens_ref[...] = dot(for_me(dens_in).astype(bf16), place).astype(dens_ref.dtype)
    wait_all(returned, back_recv)
    back = returned[...]
    mean_ref[:, :main] = dot(take, back).astype(bf16)
    mean_ref[:, main:] = sum(
        dot(take_side[g], back[:, g * side:(g + 1) * side]) for g in range(groups)
    ).astype(bf16)
    wait_sent(reply, back_send)
    wait_sent(dens_in, dens_send)


def with_kernel(sizes, cap, embeddings, row_cluster, cluster_sizes):
    devices = sizes[0] * sizes[1] * sizes[2]
    rows, width = embeddings.shape
    slots = devices * TILE
    main = width // TILE * cap
    wide = pltpu.VMEM((slots, main), bf16)
    operands = embeddings, row_cluster[None, :], cluster_sizes[None, :]
    line = pltpu.VMEM((1, slots), f32)
    lines = pltpu.VMEM((devices, 1, slots), f32)
    mean, density = pl.pallas_call(
        functools.partial(kernel, sizes, cap),
        out_shape=(
            jax.ShapeDtypeStruct((rows, width), bf16),
            jax.ShapeDtypeStruct((1, rows), f32),
        ),
        in_specs=[pl.BlockSpec(memory_space=pltpu.HBM)] * 3,
        out_specs=(pl.BlockSpec(memory_space=pltpu.VMEM),) * 2,
        scratch_shapes=[
            pltpu.VMEM((rows, width), bf16),
            pltpu.VMEM((1, rows), i32),
            pltpu.VMEM((1, cluster_sizes.shape[0]), i32),
        ]
        + [wide, wide, wide, wide, line, lines, line, lines]
        + [pltpu.SemaphoreType.DMA] * 11,
        compiler_params=pltpu.CompilerParams(
            collective_id=0, has_side_effects=True, vmem_limit_bytes=32 * 1024 * 1024
        ),
    )(*(pltpu.with_memory_space_constraint(a, pltpu.HBM) for a in operands))
    return mean, density[0].astype(bf16)


def with_exchange(sizes, cap, embeddings, row_cluster, cluster_sizes):
    axes = ("shard", "blk", "rep")
    members = sizes[1] * sizes[2]
    devices = sizes[0] * members
    slots = devices * cap
    owner = row_cluster // CLU_SUB * members + row_cluster % members
    same = owner[:, None] == owner[None, :]
    position = jnp.arange(owner.shape[0], dtype=i32)
    rank = jnp.sum((same & (position[None, :] < position[:, None])).astype(i32), axis=1)
    placing = (owner * cap + rank)[None, :] == jnp.arange(slots, dtype=i32)[:, None]
    packed = dot(placing.astype(bf16), embeddings).astype(bf16)
    packed_ids = jnp.sum(jnp.where(placing, row_cluster[None, :] + 1, 0), axis=1) - 1

    def exchange(array):
        return lax.all_to_all(array, axes, split_axis=0, concat_axis=0, tiled=True)

    docs, ids = exchange(packed), exchange(packed_ids)
    wide = docs.astype(f32)
    scale = lax.rsqrt(jnp.sum(wide * wide, axis=1) + tiny_eps)
    cosine = dot(docs, docs, ((1,), (1,))) * scale[:, None] * scale[None, :]
    matched = (ids[:, None] == ids[None, :]) & (ids[None, :] >= 0)
    values = jnp.where(matched, jnp.exp(temper * (cosine - 1.0)), 0.0)
    hits = ids[:, None] == jnp.arange(cluster_sizes.shape[0], dtype=i32)[None, :]
    size = jnp.sum(jnp.where(hits, cluster_sizes[None, :], 0), axis=1)
    size = jnp.where(ids >= 0, size, 1).astype(f32)
    density = (jnp.sum(values, axis=1) * (unit_count / size)).astype(bf16)
    weights = (values * density.astype(f32)[None, :]).astype(bf16)
    denominator = jnp.sum(weights.astype(f32), axis=1)
    denominator = jnp.where(ids >= 0, denominator, 1.0)
    mean = (dot(weights, docs) / denominator[:, None]).astype(bf16)
    back, back_density = exchange(mean), exchange(density)
    rows_out = dot(placing.astype(bf16), back, ((0,), (0,))).astype(bf16)
    density_out = jnp.sum(jnp.where(placing, back_density.astype(f32)[:, None], 0.0), axis=0)
    return rows_out, density_out.astype(bf16)


def on_device(sizes, embeddings, row_cluster, cluster_sizes):
    rows, width = embeddings.shape
    devices = sizes[0] * sizes[1] * sizes[2]
    cap = -(-3 * rows // (2 * devices))
    spare = TILE - cap
    foldable = spare > 0 and cap % spare == 0 and width * spare % (TILE * 128) == 0
    small = devices & (devices - 1) == 0 and devices <= 32
    run = with_kernel if foldable and small else with_exchange
    return run(sizes, cap, embeddings, row_cluster, cluster_sizes)


def solution(mesh):
    sizes = tuple(mesh.shape[name] for name in ("shard", "blk", "rep"))
    return jax.shard_map(
        functools.partial(on_device, sizes),
        mesh=mesh,
        in_specs=(
            P(("parts", "shard", "blk", "rep"), None),
            P(("parts", "shard", "blk", "rep")),
            P("parts"),
        ),
        out_specs=(P(("parts", "shard", "blk", "rep"), None), P(("parts", "shard", "blk", "rep"))),
        check_vma=False,
    )
```

```python
import functools

import jax
import jax.numpy as jnp
from jax import lax
from jax.experimental import pallas as pl
from jax.experimental.pallas import tpu as pltpu
from jax.sharding import PartitionSpec as P

CLU_SUB = 64
TILE = 16

temper = 8.0
unit_count = 1024.0
tiny_eps = 1e-06

f32 = jnp.float32
bf16 = jnp.bfloat16
i32 = jnp.int32
MESH = pl.DeviceIdType.MESH


def dot(a, b, dims=((1,), (0,))):
    return lax.dot_general(a, b, (dims, ((), ())), preferred_element_type=f32)


def iota(shape, dim):
    return lax.broadcasted_iota(i32, shape, dim)


def one_hot(hits):
    return jnp.where(hits, 1.0, 0.0).astype(bf16)


def to_column(row):
    n = row.shape[1]
    eye = iota((n, n), 0) == iota((n, n), 1)
    return jnp.sum(jnp.where(eye, row, jnp.zeros_like(row)), axis=1, keepdims=True)


def to_row(column):
    n = column.shape[0]
    eye = iota((n, n), 0) == iota((n, n), 1)
    return jnp.sum(jnp.where(eye, column, jnp.zeros_like(column)), axis=0, keepdims=True)


def log2(value):
    assert value & (value - 1) == 0
    return value.bit_length() - 1


def kernel(
    sizes, cap,
    emb_hbm, ids_hbm, counts_hbm, returned, take_ref, dens_ref,
    emb_ref, ids_ref, counts_ref, packed, owned, reply, id_out, id_in, dens_out, dens_in,
    emb_in, ids_in, counts_in, id_send, id_recv, row_send, row_recv, dens_send, dens_recv, back_send, back_recv,
):
    shards, blks, reps = sizes
    members = blks * reps
    devices = shards * members
    rows, width = emb_ref.shape
    slots = devices * TILE
    spare = TILE - cap
    groups = cap // spare
    side = width // TILE * spare
    main = width - side

    shard = lax.axis_index("shard")
    member = lax.axis_index("blk") * reps + lax.axis_index("rep")
    me = shard * members + member

    def partner(step):
        other, place, at, left = 0, 1, me // reps, step
        while place < devices // reps:
            other = other + ((at + left % 2) % 2) * place
            at, left, place = at // 2, left // 2, place * 2
        return other * reps

    def device(index):
        return {"shard": index // members, "blk": index // reps % blks, "rep": index % reps}

    chips = devices // reps
    steps = list(range(chips - 1, 0, -1))
    steps = [step for pair in zip(steps, steps[chips // 2:]) for step in pair] + [chips // 2]
    rep = lax.axis_index("rep")
    others = [me // reps * reps + (rep + r) % reps for r in range(1, reps)]
    others += [partner(step) + r for r in range(reps) for step in steps]

    ids_copy = pltpu.make_async_copy(ids_hbm, ids_ref, ids_in)
    emb_copy = pltpu.make_async_copy(emb_hbm, emb_ref, emb_in)
    counts_copy = pltpu.make_async_copy(counts_hbm, counts_ref, counts_in)
    ids_copy.start()
    emb_copy.start()
    counts_copy.start()

    barrier = pltpu.get_barrier_semaphore()
    for other in others:
        pl.semaphore_signal(barrier, inc=1, device_id=device(other), device_id_type=MESH)

    def chunk(ref, index):
        return ref.at[pl.ds(pl.multiple_of(index * TILE, TILE), TILE), :]

    ids_copy.wait()
    ids = ids_ref[...]
    owner = (ids >> log2(CLU_SUB)) * members + (ids & (members - 1))
    local = (ids & (CLU_SUB - 1)) >> log2(members)
    owner_col = to_column(owner)
    earlier = iota((rows, rows), 0) < iota((rows, rows), 1)
    same = owner_col == owner
    rank = jnp.sum(jnp.where(same & earlier, 1, 0), axis=0, keepdims=True)
    rank_third = sum(jnp.where(rank >= groups * q, 1, 0) for q in range(1, spare))
    rank_group = rank - groups * rank_third
    target = owner * TILE + rank
    side_target = owner * TILE + cap + rank_third

    place = one_hot(iota((slots, rows), 0) == target)
    id_out[...] = dot((local + 1).astype(f32).astype(bf16), place, ((1,), (1,)))

    def remote(src, dst, send, recv, index):
        return pltpu.make_async_remote_copy(
            src_ref=src, dst_ref=dst, send_sem=send, recv_sem=recv,
            device_id=device(index), device_id_type=MESH,
        )

    emb_copy.wait()
    last = emb_ref[:, main:]
    slot_index = iota((slots, rows), 0)
    for g in range(groups):
        columns = slice(g * side, (g + 1) * side)
        there = one_hot(slot_index == jnp.where(rank_group == g, side_target, -1))
        both = jnp.concatenate([place, there], axis=1)
        stacked = jnp.concatenate([emb_ref[:, columns], last], axis=0)
        packed[:, columns] = dot(both, stacked).astype(bf16)
    pl.semaphore_wait(barrier, devices - 1)
    for other in others:
        remote(id_out, id_in.at[me], id_send, id_recv, other).start()
    for other in others:
        remote(chunk(packed, other), chunk(owned, me), row_send, row_recv, other).start()
    own_ids = pltpu.make_async_copy(id_out, id_in.at[me], id_recv)
    own_ids.start()
    own_rows = pltpu.make_async_copy(chunk(packed, me), chunk(owned, me), row_recv)
    own_rows.start()

    def wait_all(ref, sem):
        pltpu.make_async_copy(ref, ref, sem).wait()

    def wait_sent(ref, sem):
        part = ref.at[pl.ds(0, ref.shape[0] // devices * (devices - 1))]
        pltpu.make_async_copy(part, part, sem).wait()

    pick = one_hot(iota((slots, slots), 0) == me * TILE + (iota((slots, slots), 1) & (TILE - 1)))
    mine = iota((devices, slots), 0) == (iota((devices, slots), 1) >> log2(TILE))

    def for_me(table):
        stacked = jnp.concatenate([table[d] for d in range(devices)], axis=0).astype(bf16)
        return jnp.sum(jnp.where(mine, dot(stacked, pick), 0.0), axis=0, keepdims=True)

    wait_all(id_in, id_recv)
    slot_id = for_me(id_in)
    slot_id_col = to_column(slot_id)
    matched = (slot_id_col == slot_id) & (slot_id > 0.0)
    cluster = shard * CLU_SUB + (slot_id_col.astype(i32) - 1) * members + member
    cluster = jnp.where(slot_id_col > 0.0, cluster, -1)
    counts_copy.wait()
    counts = counts_ref[...]
    table_hits = cluster == iota((slots, counts.shape[1]), 1)
    size = jnp.sum(jnp.where(table_hits, counts, 0), axis=1, keepdims=True)
    size_factor = unit_count / jnp.where(cluster >= 0, size, 1).astype(f32)
    eye = iota((slots, slots), 0) == iota((slots, slots), 1)
    row_place = iota((slots, slots), 0) & (TILE - 1)
    same_tile = (iota((slots, slots), 0) >> log2(TILE)) == (iota((slots, slots), 1) >> log2(TILE))
    column_place = iota((slots, slots), 1) & (TILE - 1)
    unfold = [
        one_hot(same_tile & (column_place >= cap) & (row_place == (column_place - cap) * groups + g))
        for g in range(groups)
    ]
    fold = [
        one_hot(same_tile & (row_place >= cap) & (column_place == (row_place - cap) * groups + g))
        for g in range(groups)
    ]

    wait_all(owned, row_recv)
    docs = owned[...]
    docs_side = sum(
        dot(unfold[g], docs[:, g * side:(g + 1) * side]) for g in range(groups)
    ).astype(bf16)
    gram = dot(docs, docs, ((1,), (1,))) + dot(docs_side, docs_side, ((1,), (1,)))
    diagonal = jnp.where(eye, gram, 0.0)
    scale_col = lax.rsqrt(jnp.sum(diagonal, axis=1, keepdims=True) + tiny_eps)
    scale_row = lax.rsqrt(jnp.sum(diagonal, axis=0, keepdims=True) + tiny_eps)
    cosine = gram * scale_col * scale_row
    values = jnp.where(matched, jnp.exp(temper * (cosine - 1.0)), 0.0)
    density = (jnp.sum(values, axis=1, keepdims=True) * size_factor).astype(bf16).astype(f32)
    density = to_row(density)
    dens_out[...] = density
    weights = (values * density).astype(bf16)
    denominator = jnp.sum(weights.astype(f32), axis=1, keepdims=True)
    denominator = jnp.where(slot_id_col > 0.0, denominator, 1.0)
    inverse = 1.0 / denominator
    for other in others:
        remote(dens_out, dens_in.at[me], dens_send, dens_recv, other).start()
    mean_side = (dot(weights, docs_side) * inverse).astype(bf16)
    for g in range(groups):
        columns = slice(g * side, (g + 1) * side)
        mean_main = dot(weights, docs[:, columns]) * inverse
        reply[:, columns] = (mean_main + dot(fold[g], mean_side)).astype(bf16)
    for other in others:
        remote(chunk(reply, other), chunk(returned, me), back_send, back_recv, other).start()
    own_back = pltpu.make_async_copy(chunk(reply, me), chunk(returned, me), back_recv)
    own_back.start()
    own_dens = pltpu.make_async_copy(dens_out, dens_in.at[me], dens_recv)
    own_dens.start()

    target_col = to_column(target)
    side_target_col = to_column(side_target)
    group_col = to_column(rank_group)
    lane = iota((rows, slots), 1)
    take_ref[:, :slots] = one_hot(lane == target_col)
    for g in range(groups):
        here = one_hot(lane == jnp.where(group_col == g, side_target_col, -1))
        take_ref[:, (g + 1) * slots:(g + 2) * slots] = here
    wait_sent(id_in, id_send)
    wait_sent(packed, row_send)
    wait_all(dens_in, dens_recv)
    dens_ref[...] = dot(for_me(dens_in).astype(bf16), place)
    wait_all(returned, back_recv)
    wait_sent(reply, back_send)
    wait_sent(dens_in, dens_send)


def unpack(returned, take_ref, dens_row, mean_hbm, dens_ref, mean_ref, sems):
    slots, main = returned.shape
    width = mean_ref.shape[1]
    side = width - main
    dens_ref[...] = dens_row[...].astype(bf16)
    copies = []
    for g in range(main // side + 1):
        columns = slice(g * side, (g + 1) * side)
        if g < main // side:
            part = dot(take_ref[:, :slots], returned[:, columns])
        else:
            part = sum(
                dot(take_ref[:, (h + 1) * slots:(h + 2) * slots], returned[:, h * side:(h + 1) * side])
                for h in range(main // side)
            )
        mean_ref[:, columns] = part.astype(bf16)
        here = mean_ref.at[:, columns]
        copies.append(pltpu.make_async_copy(here, mean_hbm.at[:, columns], sems.at[g]))
        copies[-1].start()
    for copy in copies:
        copy.wait()


def with_kernel(sizes, cap, embeddings, row_cluster, cluster_sizes):
    devices = sizes[0] * sizes[1] * sizes[2]
    rows, width = embeddings.shape
    slots = devices * TILE
    main = width // TILE * cap
    wide = pltpu.VMEM((slots, main), bf16)
    operands = embeddings, row_cluster[None, :], cluster_sizes[None, :]
    line = pltpu.VMEM((1, slots), f32)
    lines = pltpu.VMEM((devices, 1, slots), f32)
    vmem, hbm = (pl.BlockSpec(memory_space=m) for m in (pltpu.VMEM, pltpu.HBM))
    groups = main // (width - main)
    returned, take, density = pl.pallas_call(
        functools.partial(kernel, sizes, cap),
        out_shape=(
            jax.ShapeDtypeStruct((slots, main), bf16),
            jax.ShapeDtypeStruct((rows, (groups + 1) * slots), bf16),
            jax.ShapeDtypeStruct((1, rows), f32),
        ),
        in_specs=[hbm] * 3,
        out_specs=(vmem,) * 3,
        scratch_shapes=[
            pltpu.VMEM((rows, width), bf16),
            pltpu.VMEM((1, rows), i32),
            pltpu.VMEM((1, cluster_sizes.shape[0]), i32),
        ]
        + [wide, wide, wide, line, lines, line, lines]
        + [pltpu.SemaphoreType.DMA] * 11,
        compiler_params=pltpu.CompilerParams(
            collective_id=0, has_side_effects=True, vmem_limit_bytes=32 * 1024 * 1024
        ),
    )(*(pltpu.with_memory_space_constraint(a, pltpu.HBM) for a in operands))
    mean, density = pl.pallas_call(
        unpack,
        out_shape=(
            jax.ShapeDtypeStruct((rows, width), bf16),
            jax.ShapeDtypeStruct((1, rows), bf16),
        ),
        in_specs=[vmem] * 3,
        out_specs=(hbm, vmem),
        scratch_shapes=[pltpu.VMEM((rows, width), bf16), pltpu.SemaphoreType.DMA((groups + 1,))],
        compiler_params=pltpu.CompilerParams(vmem_limit_bytes=16 * 1024 * 1024),
    )(returned, take, density)
    return mean, density[0]


def with_exchange(sizes, cap, embeddings, row_cluster, cluster_sizes):
    axes = ("shard", "blk", "rep")
    members = sizes[1] * sizes[2]
    devices = sizes[0] * members
    slots = devices * cap
    owner = row_cluster // CLU_SUB * members + row_cluster % members
    same = owner[:, None] == owner[None, :]
    position = jnp.arange(owner.shape[0], dtype=i32)
    rank = jnp.sum((same & (position[None, :] < position[:, None])).astype(i32), axis=1)
    placing = (owner * cap + rank)[None, :] == jnp.arange(slots, dtype=i32)[:, None]
    packed = dot(placing.astype(bf16), embeddings).astype(bf16)
    packed_ids = jnp.sum(jnp.where(placing, row_cluster[None, :] + 1, 0), axis=1) - 1

    def exchange(array):
        return lax.all_to_all(array, axes, split_axis=0, concat_axis=0, tiled=True)

    docs, ids = exchange(packed), exchange(packed_ids)
    wide = docs.astype(f32)
    scale = lax.rsqrt(jnp.sum(wide * wide, axis=1) + tiny_eps)
    cosine = dot(docs, docs, ((1,), (1,))) * scale[:, None] * scale[None, :]
    matched = (ids[:, None] == ids[None, :]) & (ids[None, :] >= 0)
    values = jnp.where(matched, jnp.exp(temper * (cosine - 1.0)), 0.0)
    hits = ids[:, None] == jnp.arange(cluster_sizes.shape[0], dtype=i32)[None, :]
    size = jnp.sum(jnp.where(hits, cluster_sizes[None, :], 0), axis=1)
    size = jnp.where(ids >= 0, size, 1).astype(f32)
    density = (jnp.sum(values, axis=1) * (unit_count / size)).astype(bf16)
    weights = (values * density.astype(f32)[None, :]).astype(bf16)
    denominator = jnp.sum(weights.astype(f32), axis=1)
    denominator = jnp.where(ids >= 0, denominator, 1.0)
    mean = (dot(weights, docs) / denominator[:, None]).astype(bf16)
    back, back_density = exchange(mean), exchange(density)
    rows_out = dot(placing.astype(bf16), back, ((0,), (0,))).astype(bf16)
    density_out = jnp.sum(jnp.where(placing, back_density.astype(f32)[:, None], 0.0), axis=0)
    return rows_out, density_out.astype(bf16)


def on_device(sizes, embeddings, row_cluster, cluster_sizes):
    rows, width = embeddings.shape
    devices = sizes[0] * sizes[1] * sizes[2]
    cap = -(-3 * rows // (2 * devices))
    spare = TILE - cap
    foldable = spare > 0 and cap % spare == 0 and width * spare % (TILE * 128) == 0
    small = devices & (devices - 1) == 0 and devices <= 32
    run = with_kernel if foldable and small else with_exchange
    return run(sizes, cap, embeddings, row_cluster, cluster_sizes)


def solution(mesh):
    sizes = tuple(mesh.shape[name] for name in ("shard", "blk", "rep"))
    return jax.shard_map(
        functools.partial(on_device, sizes),
        mesh=mesh,
        in_specs=(
            P(("parts", "shard", "blk", "rep"), None),
            P(("parts", "shard", "blk", "rep")),
            P("parts"),
        ),
        out_specs=(P(("parts", "shard", "blk", "rep"), None), P(("parts", "shard", "blk", "rep"))),
        check_vma=False,
    )
```

```python
import functools

import jax
import jax.numpy as jnp
from jax import lax
from jax.experimental import pallas as pl
from jax.experimental.pallas import tpu as pltpu
from jax.sharding import PartitionSpec as P

CLU_SUB = 64
TILE = 16

temper = 8.0
unit_count = 1024.0
tiny_eps = 1e-06

f32 = jnp.float32
bf16 = jnp.bfloat16
i32 = jnp.int32
MESH = pl.DeviceIdType.MESH


def dot(a, b, dims=((1,), (0,))):
    return lax.dot_general(a, b, (dims, ((), ())), preferred_element_type=f32)


def iota(shape, dim):
    return lax.broadcasted_iota(i32, shape, dim)


def one_hot(hits):
    return jnp.where(hits, 1.0, 0.0).astype(bf16)


def to_column(row):
    n = row.shape[1]
    eye = iota((n, n), 0) == iota((n, n), 1)
    return jnp.sum(jnp.where(eye, row, jnp.zeros_like(row)), axis=1, keepdims=True)


def to_row(column):
    n = column.shape[0]
    eye = iota((n, n), 0) == iota((n, n), 1)
    return jnp.sum(jnp.where(eye, column, jnp.zeros_like(column)), axis=0, keepdims=True)


def log2(value):
    assert value & (value - 1) == 0
    return value.bit_length() - 1


def kernel(
    sizes, cap,
    emb_hbm, ids_hbm, counts_hbm, mean_ref, dens_ref,
    emb_ref, ids_ref, counts_ref, packed, owned, reply, returned, id_out, id_in, dens_out, dens_in,
    emb_in, ids_in, counts_in, id_send, id_recv, row_send, row_recv, dens_send, dens_recv, back_send, back_recv, late_sem,
):
    shards, blks, reps = sizes
    members = blks * reps
    devices = shards * members
    rows, width = emb_ref.shape
    slots = devices * TILE
    spare = TILE - cap
    groups = cap // spare
    side = width // TILE * spare
    main = width - side

    shard = lax.axis_index("shard")
    member = lax.axis_index("blk") * reps + lax.axis_index("rep")
    me = shard * members + member

    def device(index):
        return {"shard": index // members, "blk": index // reps % blks, "rep": index % reps}

    blk, rep = lax.axis_index("blk"), lax.axis_index("rep")
    first, second, third = 2 - shard // 2, 1 - (shard + 2) // 3, 3 - shard // 3

    def towards(other_shard, r):
        return [(other_shard * blks + (blk + k) % blks) * reps + r for k in range(blks)]

    beside = [me // reps * reps + (rep + r) % reps for r in range(1, reps)]
    around = [
        [(shard * blks + (blk + k) % blks) * reps + r for k in range(1, blks)] for r in range(reps)
    ]
    early = [
        [x for pair in zip(towards(first, r), towards(second, r)) for x in pair] + around[r]
        for r in range(reps)
    ]
    late = [towards(third, r) for r in range(reps)]
    others = beside + [x for r in range(reps) for x in early[r] + late[r]]
    across = [x for r in range(reps) for z in (first, second, third) for x in towards(z, r)]
    is_last = shard == shards - 1

    ids_copy = pltpu.make_async_copy(ids_hbm, ids_ref, ids_in)
    emb_copy = pltpu.make_async_copy(emb_hbm, emb_ref, emb_in)
    counts_copy = pltpu.make_async_copy(counts_hbm, counts_ref, counts_in)
    ids_copy.start()
    emb_copy.start()
    counts_copy.start()

    barrier = pltpu.get_barrier_semaphore()
    for other in beside + [x for r in range(reps) for x in around[r]]:
        pl.semaphore_signal(barrier, inc=1, device_id=device(other), device_id_type=MESH)

    @pl.when(shard < shards - 1)
    def _():
        for other in across:
            pl.semaphore_signal(barrier, inc=1, device_id=device(other), device_id_type=MESH)

    @pl.when(is_last)
    def _():
        pl.semaphore_wait(barrier, devices - 1)
        for other in across:
            pl.semaphore_signal(late_sem, inc=1, device_id=device(other), device_id_type=MESH)

    def chunk(ref, index):
        return ref.at[pl.ds(pl.multiple_of(index * TILE, TILE), TILE), :]

    ids_copy.wait()
    ids = ids_ref[...]
    owner = (ids >> log2(CLU_SUB)) * members + (ids & (members - 1))
    local = (ids & (CLU_SUB - 1)) >> log2(members)
    owner_col = to_column(owner)
    earlier = iota((rows, rows), 0) < iota((rows, rows), 1)
    same = owner_col == owner
    rank = jnp.sum(jnp.where(same & earlier, 1, 0), axis=0, keepdims=True)
    rank_third = sum(jnp.where(rank >= groups * q, 1, 0) for q in range(1, spare))
    rank_group = rank - groups * rank_third
    target = owner * TILE + rank
    side_target = owner * TILE + cap + rank_third

    place = one_hot(iota((slots, rows), 0) == target)
    id_out[...] = dot((local + 1).astype(f32).astype(bf16), place, ((1,), (1,)))

    def remote(src, dst, send, recv, index):
        return pltpu.make_async_remote_copy(
            src_ref=src, dst_ref=dst, send_sem=send, recv_sem=recv,
            device_id=device(index), device_id_type=MESH,
        )

    emb_copy.wait()
    last = emb_ref[:, main:]
    slot_index = iota((slots, rows), 0)
    for g in range(groups):
        columns = slice(g * side, (g + 1) * side)
        there = one_hot(slot_index == jnp.where(rank_group == g, side_target, -1))
        both = jnp.concatenate([place, there], axis=1)
        stacked = jnp.concatenate([emb_ref[:, columns], last], axis=0)
        packed[:, columns] = dot(both, stacked).astype(bf16)

    @pl.when(shard < shards - 1)
    def _():
        pl.semaphore_wait(barrier, devices - 1 - members)

    def send_ids(targets):
        for other in targets:
            remote(id_out, id_in.at[me], id_send, id_recv, other).start()

    def send_rows(targets):
        for other in targets:
            remote(chunk(packed, other), chunk(owned, me), row_send, row_recv, other).start()

    send_ids(beside + [x for r in range(reps) for x in early[r]])
    send_rows(beside + early[0])

    @pl.when(shard < shards - 1)
    def _():
        pl.semaphore_wait(late_sem, members)

    send_ids([x for r in range(reps) for x in late[r]])
    send_rows(late[0])
    for r in range(1, reps):
        send_rows(early[r] + late[r])
    own_ids = pltpu.make_async_copy(id_out, id_in.at[me], id_recv)
    own_ids.start()
    own_rows = pltpu.make_async_copy(chunk(packed, me), chunk(owned, me), row_recv)
    own_rows.start()

    def wait_all(ref, sem):
        pltpu.make_async_copy(ref, ref, sem).wait()

    def wait_sent(ref, sem):
        part = ref.at[pl.ds(0, ref.shape[0] // devices * (devices - 1))]
        pltpu.make_async_copy(part, part, sem).wait()

    pick = one_hot(iota((slots, slots), 0) == me * TILE + (iota((slots, slots), 1) & (TILE - 1)))
    mine = iota((devices, slots), 0) == (iota((devices, slots), 1) >> log2(TILE))

    def for_me(table):
        stacked = jnp.concatenate([table[d] for d in range(devices)], axis=0).astype(bf16)
        return jnp.sum(jnp.where(mine, dot(stacked, pick), 0.0), axis=0, keepdims=True)

    wait_all(id_in, id_recv)
    slot_id = for_me(id_in)
    slot_id_col = to_column(slot_id)
    matched = (slot_id_col == slot_id) & (slot_id > 0.0)
    cluster = shard * CLU_SUB + (slot_id_col.astype(i32) - 1) * members + member
    cluster = jnp.where(slot_id_col > 0.0, cluster, -1)
    counts_copy.wait()
    counts = counts_ref[...]
    table_hits = cluster == iota((slots, counts.shape[1]), 1)
    size = jnp.sum(jnp.where(table_hits, counts, 0), axis=1, keepdims=True)
    size_factor = unit_count / jnp.where(cluster >= 0, size, 1).astype(f32)
    eye = iota((slots, slots), 0) == iota((slots, slots), 1)
    row_place = iota((slots, slots), 0) & (TILE - 1)
    same_tile = (iota((slots, slots), 0) >> log2(TILE)) == (iota((slots, slots), 1) >> log2(TILE))
    column_place = iota((slots, slots), 1) & (TILE - 1)
    unfold = [
        one_hot(same_tile & (column_place >= cap) & (row_place == (column_place - cap) * groups + g))
        for g in range(groups)
    ]
    fold = [
        one_hot(same_tile & (row_place >= cap) & (column_place == (row_place - cap) * groups + g))
        for g in range(groups)
    ]

    wait_all(owned, row_recv)
    docs = owned[...]
    docs_side = sum(
        dot(unfold[g], docs[:, g * side:(g + 1) * side]) for g in range(groups)
    ).astype(bf16)
    gram = dot(docs, docs, ((1,), (1,))) + dot(docs_side, docs_side, ((1,), (1,)))
    diagonal = jnp.where(eye, gram, 0.0)
    scale_col = lax.rsqrt(jnp.sum(diagonal, axis=1, keepdims=True) + tiny_eps)
    scale_row = lax.rsqrt(jnp.sum(diagonal, axis=0, keepdims=True) + tiny_eps)
    cosine = gram * scale_col * scale_row
    values = jnp.where(matched, jnp.exp(temper * (cosine - 1.0)), 0.0)
    density = (jnp.sum(values, axis=1, keepdims=True) * size_factor).astype(bf16).astype(f32)
    density = to_row(density)
    dens_out[...] = density
    weights = (values * density).astype(bf16)
    denominator = jnp.sum(weights.astype(f32), axis=1, keepdims=True)
    denominator = jnp.where(slot_id_col > 0.0, denominator, 1.0)
    inverse = 1.0 / denominator
    for other in others:
        remote(dens_out, dens_in.at[me], dens_send, dens_recv, other).start()
    mean_side = (dot(weights, docs_side) * inverse).astype(bf16)
    for g in range(groups):
        columns = slice(g * side, (g + 1) * side)
        mean_main = dot(weights, docs[:, columns]) * inverse
        reply[:, columns] = (mean_main + dot(fold[g], mean_side)).astype(bf16)
    for other in others:
        remote(chunk(reply, other), chunk(returned, me), back_send, back_recv, other).start()
    own_back = pltpu.make_async_copy(chunk(reply, me), chunk(returned, me), back_recv)
    own_back.start()
    own_dens = pltpu.make_async_copy(dens_out, dens_in.at[me], dens_recv)
    own_dens.start()

    target_col = to_column(target)
    side_target_col = to_column(side_target)
    group_col = to_column(rank_group)
    lane = iota((rows, slots), 1)
    take = one_hot(lane == target_col)
    take_side = [
        one_hot(lane == jnp.where(group_col == g, side_target_col, -1)) for g in range(groups)
    ]
    wait_sent(id_in, id_send)
    wait_sent(packed, row_send)
    wait_all(dens_in, dens_recv)
    dens_ref[...] = dot(for_me(dens_in).astype(bf16), place).astype(dens_ref.dtype)
    wait_all(returned, back_recv)
    back = returned[...]
    mean_ref[:, :main] = dot(take, back).astype(bf16)
    mean_ref[:, main:] = sum(
        dot(take_side[g], back[:, g * side:(g + 1) * side]) for g in range(groups)
    ).astype(bf16)
    wait_sent(reply, back_send)
    wait_sent(dens_in, dens_send)


def hand_out(mean_ref, dens_row, mean_hbm, dens_hbm, dens_ref, mean_sem, dens_sem):
    mean_copy = pltpu.make_async_copy(mean_ref, mean_hbm, mean_sem)
    mean_copy.start()
    dens_ref[...] = dens_row[...].astype(bf16)
    dens_copy = pltpu.make_async_copy(dens_ref, dens_hbm, dens_sem)
    dens_copy.start()
    dens_copy.wait()
    mean_copy.wait()


def with_kernel(sizes, cap, embeddings, row_cluster, cluster_sizes):
    devices = sizes[0] * sizes[1] * sizes[2]
    rows, width = embeddings.shape
    slots = devices * TILE
    main = width // TILE * cap
    wide = pltpu.VMEM((slots, main), bf16)
    operands = embeddings, row_cluster[None, :], cluster_sizes[None, :]
    line = pltpu.VMEM((1, slots), f32)
    lines = pltpu.VMEM((devices, 1, slots), f32)
    vmem, hbm = (pl.BlockSpec(memory_space=m) for m in (pltpu.VMEM, pltpu.HBM))
    mean, density = pl.pallas_call(
        functools.partial(kernel, sizes, cap),
        out_shape=(
            jax.ShapeDtypeStruct((rows, width), bf16),
            jax.ShapeDtypeStruct((1, rows), f32),
        ),
        in_specs=[hbm] * 3,
        out_specs=(vmem,) * 2,
        scratch_shapes=[
            pltpu.VMEM((rows, width), bf16),
            pltpu.VMEM((1, rows), i32),
            pltpu.VMEM((1, cluster_sizes.shape[0]), i32),
        ]
        + [wide, wide, wide, wide, line, lines, line, lines]
        + [pltpu.SemaphoreType.DMA] * 11
        + [pltpu.SemaphoreType.REGULAR],
        compiler_params=pltpu.CompilerParams(
            collective_id=0, has_side_effects=True, vmem_limit_bytes=32 * 1024 * 1024
        ),
    )(*(pltpu.with_memory_space_constraint(a, pltpu.HBM) for a in operands))
    mean, density = pl.pallas_call(
        hand_out,
        out_shape=(
            jax.ShapeDtypeStruct((rows, width), bf16),
            jax.ShapeDtypeStruct((1, rows), bf16),
        ),
        in_specs=[vmem] * 2,
        out_specs=(hbm, hbm),
        scratch_shapes=[pltpu.VMEM((1, rows), bf16)] + [pltpu.SemaphoreType.DMA] * 2,
        compiler_params=pltpu.CompilerParams(vmem_limit_bytes=16 * 1024 * 1024),
    )(mean, density)
    return mean, density[0]


def with_exchange(sizes, cap, embeddings, row_cluster, cluster_sizes):
    axes = ("shard", "blk", "rep")
    members = sizes[1] * sizes[2]
    devices = sizes[0] * members
    slots = devices * cap
    owner = row_cluster // CLU_SUB * members + row_cluster % members
    same = owner[:, None] == owner[None, :]
    position = jnp.arange(owner.shape[0], dtype=i32)
    rank = jnp.sum((same & (position[None, :] < position[:, None])).astype(i32), axis=1)
    placing = (owner * cap + rank)[None, :] == jnp.arange(slots, dtype=i32)[:, None]
    packed = dot(placing.astype(bf16), embeddings).astype(bf16)
    packed_ids = jnp.sum(jnp.where(placing, row_cluster[None, :] + 1, 0), axis=1) - 1

    def exchange(array):
        return lax.all_to_all(array, axes, split_axis=0, concat_axis=0, tiled=True)

    docs, ids = exchange(packed), exchange(packed_ids)
    wide = docs.astype(f32)
    scale = lax.rsqrt(jnp.sum(wide * wide, axis=1) + tiny_eps)
    cosine = dot(docs, docs, ((1,), (1,))) * scale[:, None] * scale[None, :]
    matched = (ids[:, None] == ids[None, :]) & (ids[None, :] >= 0)
    values = jnp.where(matched, jnp.exp(temper * (cosine - 1.0)), 0.0)
    hits = ids[:, None] == jnp.arange(cluster_sizes.shape[0], dtype=i32)[None, :]
    size = jnp.sum(jnp.where(hits, cluster_sizes[None, :], 0), axis=1)
    size = jnp.where(ids >= 0, size, 1).astype(f32)
    density = (jnp.sum(values, axis=1) * (unit_count / size)).astype(bf16)
    weights = (values * density.astype(f32)[None, :]).astype(bf16)
    denominator = jnp.sum(weights.astype(f32), axis=1)
    denominator = jnp.where(ids >= 0, denominator, 1.0)
    mean = (dot(weights, docs) / denominator[:, None]).astype(bf16)
    back, back_density = exchange(mean), exchange(density)
    rows_out = dot(placing.astype(bf16), back, ((0,), (0,))).astype(bf16)
    density_out = jnp.sum(jnp.where(placing, back_density.astype(f32)[:, None], 0.0), axis=0)
    return rows_out, density_out.astype(bf16)


def on_device(sizes, embeddings, row_cluster, cluster_sizes):
    rows, width = embeddings.shape
    devices = sizes[0] * sizes[1] * sizes[2]
    cap = -(-3 * rows // (2 * devices))
    spare = TILE - cap
    foldable = spare > 0 and cap % spare == 0 and width * spare % (TILE * 128) == 0
    small = devices & (devices - 1) == 0 and devices <= 32 and sizes[0] == 4
    run = with_kernel if foldable and small else with_exchange
    return run(sizes, cap, embeddings, row_cluster, cluster_sizes)


def solution(mesh):
    sizes = tuple(mesh.shape[name] for name in ("shard", "blk", "rep"))
    return jax.shard_map(
        functools.partial(on_device, sizes),
        mesh=mesh,
        in_specs=(
            P(("parts", "shard", "blk", "rep"), None),
            P(("parts", "shard", "blk", "rep")),
            P("parts"),
        ),
        out_specs=(P(("parts", "shard", "blk", "rep"), None), P(("parts", "shard", "blk", "rep"))),
        check_vma=False,
    )
```

```python
import functools

import jax
import jax.numpy as jnp
from jax import lax
from jax.experimental import pallas as pl
from jax.experimental.pallas import tpu as pltpu
from jax.sharding import PartitionSpec as P

CLU_SUB = 64
TILE = 16

temper = 8.0
unit_count = 1024.0
tiny_eps = 1e-06

f32 = jnp.float32
bf16 = jnp.bfloat16
i32 = jnp.int32
MESH = pl.DeviceIdType.MESH


def dot(a, b, dims=((1,), (0,))):
    return lax.dot_general(a, b, (dims, ((), ())), preferred_element_type=f32)


def iota(shape, dim):
    return lax.broadcasted_iota(i32, shape, dim)


def one_hot(hits):
    return jnp.where(hits, 1.0, 0.0).astype(bf16)


def to_column(row):
    n = row.shape[1]
    eye = iota((n, n), 0) == iota((n, n), 1)
    return jnp.sum(jnp.where(eye, row, jnp.zeros_like(row)), axis=1, keepdims=True)


def to_row(column):
    n = column.shape[0]
    eye = iota((n, n), 0) == iota((n, n), 1)
    return jnp.sum(jnp.where(eye, column, jnp.zeros_like(column)), axis=0, keepdims=True)


def log2(value):
    assert value & (value - 1) == 0
    return value.bit_length() - 1


def kernel(
    sizes, cap,
    emb_hbm, ids_hbm, counts_hbm, mean_ref, dens_ref,
    emb_ref, ids_ref, counts_ref, packed, owned, reply, returned, id_out, id_in, dens_out, dens_in,
    emb_in, ids_in, counts_in, id_send, id_recv, row_send, row_recv, dens_send, dens_recv, back_send, back_recv, late_sem,
):
    shards, blks, reps = sizes
    members = blks * reps
    devices = shards * members
    rows, width = emb_ref.shape
    slots = devices * TILE
    spare = TILE - cap
    groups = cap // spare
    side = width // TILE * spare
    main = width - side

    shard = lax.axis_index("shard")
    member = lax.axis_index("blk") * reps + lax.axis_index("rep")
    me = shard * members + member

    def device(index):
        return {"shard": index // members, "blk": index // reps % blks, "rep": index % reps}

    blk, rep = lax.axis_index("blk"), lax.axis_index("rep")
    first, second, third = 2 - shard // 2, 1 - (shard + 2) // 3, 3 - shard // 3

    def towards(other_shard, r):
        return [(other_shard * blks + (blk + k) % blks) * reps + r for k in range(blks)]

    beside = [me // reps * reps + (rep + r) % reps for r in range(1, reps)]
    around = [
        [(shard * blks + (blk + k) % blks) * reps + r for k in range(1, blks)] for r in range(reps)
    ]
    early = [
        [x for pair in zip(towards(first, r), towards(second, r)) for x in pair] + around[r]
        for r in range(reps)
    ]
    late = [towards(third, r) for r in range(reps)]
    others = beside + [x for r in range(reps) for x in early[r] + late[r]]
    across = [x for r in range(reps) for z in (first, second, third) for x in towards(z, r)]
    is_last = shard == shards - 1

    ids_copy = pltpu.make_async_copy(ids_hbm, ids_ref, ids_in)
    emb_copy = pltpu.make_async_copy(emb_hbm, emb_ref, emb_in)
    counts_copy = pltpu.make_async_copy(counts_hbm, counts_ref, counts_in)
    ids_copy.start()
    emb_copy.start()
    counts_copy.start()

    barrier = pltpu.get_barrier_semaphore()
    for other in beside + [x for r in range(reps) for x in around[r]]:
        pl.semaphore_signal(barrier, inc=1, device_id=device(other), device_id_type=MESH)

    @pl.when(shard < shards - 1)
    def _():
        for other in across:
            pl.semaphore_signal(barrier, inc=1, device_id=device(other), device_id_type=MESH)

    @pl.when(is_last)
    def _():
        pl.semaphore_wait(barrier, devices - 1)
        for other in across:
            pl.semaphore_signal(late_sem, inc=1, device_id=device(other), device_id_type=MESH)

    def chunk(ref, index):
        return ref.at[pl.ds(pl.multiple_of(index * TILE, TILE), TILE), :]

    ids_copy.wait()
    ids = ids_ref[...]
    owner = (ids >> log2(CLU_SUB)) * members + (ids & (members - 1))
    local = (ids & (CLU_SUB - 1)) >> log2(members)
    owner_col = to_column(owner)
    earlier = iota((rows, rows), 0) < iota((rows, rows), 1)
    same = owner_col == owner
    rank = jnp.sum(jnp.where(same & earlier, 1, 0), axis=0, keepdims=True)
    rank_third = sum(jnp.where(rank >= groups * q, 1, 0) for q in range(1, spare))
    rank_group = rank - groups * rank_third
    target = owner * TILE + rank
    side_target = owner * TILE + cap + rank_third

    place = one_hot(iota((slots, rows), 0) == target)
    id_out[...] = dot((local + 1).astype(f32).astype(bf16), place, ((1,), (1,)))

    def remote(src, dst, send, recv, index):
        return pltpu.make_async_remote_copy(
            src_ref=src, dst_ref=dst, send_sem=send, recv_sem=recv,
            device_id=device(index), device_id_type=MESH,
        )

    emb_copy.wait()
    last = emb_ref[:, main:]
    slot_index = iota((slots, rows), 0)
    for g in range(groups):
        columns = slice(g * side, (g + 1) * side)
        there = one_hot(slot_index == jnp.where(rank_group == g, side_target, -1))
        both = jnp.concatenate([place, there], axis=1)
        stacked = jnp.concatenate([emb_ref[:, columns], last], axis=0)
        packed[:, columns] = dot(both, stacked).astype(bf16)

    @pl.when(shard < shards - 1)
    def _():
        pl.semaphore_wait(barrier, devices - 1 - members)

    def send_ids(targets):
        for other in targets:
            remote(id_out, id_in.at[me], id_send, id_recv, other).start()

    def send_rows(targets):
        for other in targets:
            remote(chunk(packed, other), chunk(owned, me), row_send, row_recv, other).start()

    send_ids(beside + [x for r in range(reps) for x in early[r]])
    send_rows(beside + early[0])

    @pl.when(shard < shards - 1)
    def _():
        pl.semaphore_wait(late_sem, members)

    send_ids([x for r in range(reps) for x in late[r]])
    send_rows(late[0])
    for r in range(1, reps):
        send_rows(early[r] + late[r])
    own_ids = pltpu.make_async_copy(id_out, id_in.at[me], id_recv)
    own_ids.start()
    own_rows = pltpu.make_async_copy(chunk(packed, me), chunk(owned, me), row_recv)
    own_rows.start()

    def wait_all(ref, sem):
        pltpu.make_async_copy(ref, ref, sem).wait()

    def wait_sent(ref, sem):
        part = ref.at[pl.ds(0, ref.shape[0] // devices * (devices - 1))]
        pltpu.make_async_copy(part, part, sem).wait()

    pick = one_hot(iota((slots, slots), 0) == me * TILE + (iota((slots, slots), 1) & (TILE - 1)))
    mine = iota((devices, slots), 0) == (iota((devices, slots), 1) >> log2(TILE))

    def for_me(table):
        stacked = jnp.concatenate([table[d] for d in range(devices)], axis=0).astype(bf16)
        return jnp.sum(jnp.where(mine, dot(stacked, pick), 0.0), axis=0, keepdims=True)

    wait_all(id_in, id_recv)
    slot_id = for_me(id_in)
    slot_id_col = to_column(slot_id)
    matched = (slot_id_col == slot_id) & (slot_id > 0.0)
    cluster = shard * CLU_SUB + (slot_id_col.astype(i32) - 1) * members + member
    cluster = jnp.where(slot_id_col > 0.0, cluster, -1)
    counts_copy.wait()
    counts = counts_ref[...]
    table_hits = cluster == iota((slots, counts.shape[1]), 1)
    size = jnp.sum(jnp.where(table_hits, counts, 0), axis=1, keepdims=True)
    size_factor = unit_count / jnp.where(cluster >= 0, size, 1).astype(f32)
    eye = iota((slots, slots), 0) == iota((slots, slots), 1)
    row_place = iota((slots, slots), 0) & (TILE - 1)
    same_tile = (iota((slots, slots), 0) >> log2(TILE)) == (iota((slots, slots), 1) >> log2(TILE))
    column_place = iota((slots, slots), 1) & (TILE - 1)
    unfold = [
        one_hot(same_tile & (column_place >= cap) & (row_place == (column_place - cap) * groups + g))
        for g in range(groups)
    ]
    fold = [
        one_hot(same_tile & (row_place >= cap) & (column_place == (row_place - cap) * groups + g))
        for g in range(groups)
    ]

    wait_all(owned, row_recv)
    docs = owned[...]
    docs_side = sum(
        dot(unfold[g], docs[:, g * side:(g + 1) * side]) for g in range(groups)
    ).astype(bf16)
    gram = dot(docs, docs, ((1,), (1,))) + dot(docs_side, docs_side, ((1,), (1,)))
    diagonal = jnp.where(eye, gram, 0.0)
    scale_col = lax.rsqrt(jnp.sum(diagonal, axis=1, keepdims=True) + tiny_eps)
    scale_row = lax.rsqrt(jnp.sum(diagonal, axis=0, keepdims=True) + tiny_eps)
    cosine = gram * scale_col * scale_row
    values = jnp.where(matched, jnp.exp(temper * (cosine - 1.0)), 0.0)
    density = (jnp.sum(values, axis=1, keepdims=True) * size_factor).astype(bf16).astype(f32)
    density = to_row(density)
    dens_out[...] = density
    weights = (values * density).astype(bf16)
    denominator = jnp.sum(weights.astype(f32), axis=1, keepdims=True)
    denominator = jnp.where(slot_id_col > 0.0, denominator, 1.0)
    inverse = 1.0 / denominator
    for other in others:
        remote(dens_out, dens_in.at[me], dens_send, dens_recv, other).start()
    mean_side = (dot(weights, docs_side) * inverse).astype(bf16)
    for g in range(groups):
        columns = slice(g * side, (g + 1) * side)
        mean_main = dot(weights, docs[:, columns]) * inverse
        reply[:, columns] = (mean_main + dot(fold[g], mean_side)).astype(bf16)
    near, far = ([x for r in range(reps) for x in towards(z, r)] for z in (second, first))
    answers = near + far
    answers += beside + [x for r in range(reps) for x in around[r]]
    answers += [x for r in range(reps) for x in late[r]]
    for other in answers:
        remote(chunk(reply, other), chunk(returned, me), back_send, back_recv, other).start()
    own_back = pltpu.make_async_copy(chunk(reply, me), chunk(returned, me), back_recv)
    own_back.start()
    own_dens = pltpu.make_async_copy(dens_out, dens_in.at[me], dens_recv)
    own_dens.start()

    target_col = to_column(target)
    side_target_col = to_column(side_target)
    group_col = to_column(rank_group)
    lane = iota((rows, slots), 1)
    take = one_hot(lane == target_col)
    take_side = [
        one_hot(lane == jnp.where(group_col == g, side_target_col, -1)) for g in range(groups)
    ]
    wait_sent(id_in, id_send)
    wait_sent(packed, row_send)
    wait_all(dens_in, dens_recv)
    dens_ref[...] = dot(for_me(dens_in).astype(bf16), place).astype(dens_ref.dtype)
    wait_all(returned, back_recv)
    back = returned[...]
    mean_ref[:, :main] = dot(take, back).astype(bf16)
    mean_ref[:, main:] = sum(
        dot(take_side[g], back[:, g * side:(g + 1) * side]) for g in range(groups)
    ).astype(bf16)
    wait_sent(reply, back_send)
    wait_sent(dens_in, dens_send)


def hand_out(mean_ref, dens_row, mean_hbm, dens_hbm, dens_ref, mean_sem, dens_sem):
    mean_copy = pltpu.make_async_copy(mean_ref, mean_hbm, mean_sem)
    mean_copy.start()
    dens_ref[...] = dens_row[...].astype(bf16)
    dens_copy = pltpu.make_async_copy(dens_ref, dens_hbm, dens_sem)
    dens_copy.start()
    dens_copy.wait()
    mean_copy.wait()


def with_kernel(sizes, cap, embeddings, row_cluster, cluster_sizes):
    devices = sizes[0] * sizes[1] * sizes[2]
    rows, width = embeddings.shape
    slots = devices * TILE
    main = width // TILE * cap
    wide = pltpu.VMEM((slots, main), bf16)
    operands = embeddings, row_cluster[None, :], cluster_sizes[None, :]
    line = pltpu.VMEM((1, slots), f32)
    lines = pltpu.VMEM((devices, 1, slots), f32)
    vmem, hbm = (pl.BlockSpec(memory_space=m) for m in (pltpu.VMEM, pltpu.HBM))
    mean, density = pl.pallas_call(
        functools.partial(kernel, sizes, cap),
        out_shape=(
            jax.ShapeDtypeStruct((rows, width), bf16),
            jax.ShapeDtypeStruct((1, rows), f32),
        ),
        in_specs=[hbm] * 3,
        out_specs=(vmem,) * 2,
        scratch_shapes=[
            pltpu.VMEM((rows, width), bf16),
            pltpu.VMEM((1, rows), i32),
            pltpu.VMEM((1, cluster_sizes.shape[0]), i32),
        ]
        + [wide, wide, wide, wide, line, lines, line, lines]
        + [pltpu.SemaphoreType.DMA] * 11
        + [pltpu.SemaphoreType.REGULAR],
        compiler_params=pltpu.CompilerParams(
            collective_id=0, has_side_effects=True, vmem_limit_bytes=32 * 1024 * 1024
        ),
    )(*(pltpu.with_memory_space_constraint(a, pltpu.HBM) for a in operands))
    mean, density = pl.pallas_call(
        hand_out,
        out_shape=(
            jax.ShapeDtypeStruct((rows, width), bf16),
            jax.ShapeDtypeStruct((1, rows), bf16),
        ),
        in_specs=[vmem] * 2,
        out_specs=(hbm, hbm),
        scratch_shapes=[pltpu.VMEM((1, rows), bf16)] + [pltpu.SemaphoreType.DMA] * 2,
        compiler_params=pltpu.CompilerParams(vmem_limit_bytes=16 * 1024 * 1024),
    )(mean, density)
    return mean, density[0]


def with_exchange(sizes, cap, embeddings, row_cluster, cluster_sizes):
    axes = ("shard", "blk", "rep")
    members = sizes[1] * sizes[2]
    devices = sizes[0] * members
    slots = devices * cap
    owner = row_cluster // CLU_SUB * members + row_cluster % members
    same = owner[:, None] == owner[None, :]
    position = jnp.arange(owner.shape[0], dtype=i32)
    rank = jnp.sum((same & (position[None, :] < position[:, None])).astype(i32), axis=1)
    placing = (owner * cap + rank)[None, :] == jnp.arange(slots, dtype=i32)[:, None]
    packed = dot(placing.astype(bf16), embeddings).astype(bf16)
    packed_ids = jnp.sum(jnp.where(placing, row_cluster[None, :] + 1, 0), axis=1) - 1

    def exchange(array):
        return lax.all_to_all(array, axes, split_axis=0, concat_axis=0, tiled=True)

    docs, ids = exchange(packed), exchange(packed_ids)
    wide = docs.astype(f32)
    scale = lax.rsqrt(jnp.sum(wide * wide, axis=1) + tiny_eps)
    cosine = dot(docs, docs, ((1,), (1,))) * scale[:, None] * scale[None, :]
    matched = (ids[:, None] == ids[None, :]) & (ids[None, :] >= 0)
    values = jnp.where(matched, jnp.exp(temper * (cosine - 1.0)), 0.0)
    hits = ids[:, None] == jnp.arange(cluster_sizes.shape[0], dtype=i32)[None, :]
    size = jnp.sum(jnp.where(hits, cluster_sizes[None, :], 0), axis=1)
    size = jnp.where(ids >= 0, size, 1).astype(f32)
    density = (jnp.sum(values, axis=1) * (unit_count / size)).astype(bf16)
    weights = (values * density.astype(f32)[None, :]).astype(bf16)
    denominator = jnp.sum(weights.astype(f32), axis=1)
    denominator = jnp.where(ids >= 0, denominator, 1.0)
    mean = (dot(weights, docs) / denominator[:, None]).astype(bf16)
    back, back_density = exchange(mean), exchange(density)
    rows_out = dot(placing.astype(bf16), back, ((0,), (0,))).astype(bf16)
    density_out = jnp.sum(jnp.where(placing, back_density.astype(f32)[:, None], 0.0), axis=0)
    return rows_out, density_out.astype(bf16)


def on_device(sizes, embeddings, row_cluster, cluster_sizes):
    rows, width = embeddings.shape
    devices = sizes[0] * sizes[1] * sizes[2]
    cap = -(-3 * rows // (2 * devices))
    spare = TILE - cap
    foldable = spare > 0 and cap % spare == 0 and width * spare % (TILE * 128) == 0
    small = devices & (devices - 1) == 0 and devices <= 32 and sizes[0] == 4
    run = with_kernel if foldable and small else with_exchange
    return run(sizes, cap, embeddings, row_cluster, cluster_sizes)


def solution(mesh):
    sizes = tuple(mesh.shape[name] for name in ("shard", "blk", "rep"))
    return jax.shard_map(
        functools.partial(on_device, sizes),
        mesh=mesh,
        in_specs=(
            P(("parts", "shard", "blk", "rep"), None),
            P(("parts", "shard", "blk", "rep")),
            P("parts"),
        ),
        out_specs=(P(("parts", "shard", "blk", "rep"), None), P(("parts", "shard", "blk", "rep"))),
        check_vma=False,
    )
```
